256 devices in a mesh: seq: 64 (over z_lo, y, x, core), grp: 4 (over z_hi).
Axes of the slice: x: 4, y: 4, z: 8 (z_hi: 4, z_lo: 2; z = z_hi * 2 + z_lo), core: 2. Of those that a mesh axis runs over, the one named last changes fastest.
Arguments:
- candidates: bfloat16 [64, 128, 128], P('grp', 'seq'), may hold values from -6 to 6
- behav_keys: bfloat16 [64, 65536, 128], P('grp', 'seq'), may hold values from -100 to 100
- behav_values: bfloat16 [64, 65536, 128], P('grp', 'seq'), may hold values from -6 to 6
- w_query: bfloat16 [128, 128], replicated, may hold values from -0.5 to 0.5
- w_hidden: bfloat16 [256, 1024], replicated, may hold values from -0.375 to 0.375
- w_out: float32 [1024], replicated, may hold values from -0.1875 to 0.1875
- clicks: int32 [64, 128], P('grp', 'seq'), may hold values 0 or 1
Outputs:
- logits: float32 [64, 128], P('grp', 'seq')
- grad_hidden: float32 [256, 1024], replicated
- grad_out: float32 [1024], replicated
The draws below stay inside these ranges and needn't reach their ends.
All inputs are finite; a program needn't handle non-finite values. No bound on the sum of `clicks` on one device may be relied on, other than what follows from the above.
Results may differ from the reference program's by a relative error of at most 0.0065.
The reference program's roundings to bfloat16 on the way (of `queries`, `probs`, `attended`, `features`, `hidden` and `dpre`) count: a program that leaves them out, or rounds other values in their place, can miss the bound.
Values may be sent and summed in bfloat16 or wider, within the bound.
A program may use at most 64 MiB of HBM per device.

```python
import jax
import jax.numpy as jnp
from jax import lax

D = 128
HEADS = 4
HEAD = 32
HID = 1024
CANDS = 128
L_DEV = 1024
USERS = 64
LENGTH = 65536
N_SEQ = 64


def draw_behav_keys(key, part):
    key = jax.random.fold_in(key, 7)
    base_key = jax.random.fold_in(key, 0)
    base = 3.0 * jnp.clip(jax.random.normal(base_key, (USERS, LENGTH, D), jnp.float32), -5.0, 5.0)
    return base.astype(jnp.bfloat16)


def draw_behav_values(key, part):
    key = jax.random.fold_in(key, 11)
    mean_key, noise_key = jax.random.split(key, 2)
    centre = 0.5 * jnp.clip(jax.random.normal(mean_key, (USERS, 1, D), jnp.float32), -3.0, 3.0)
    noise = 0.8 * jnp.clip(jax.random.normal(noise_key, (USERS, LENGTH, D), jnp.float32), -5.0, 5.0)
    return (centre + noise).astype(jnp.bfloat16)


def with_ends(array, key, least, high):
    place = [jax.random.randint(jax.random.fold_in(key, axis), (), 0, length) for axis, length in enumerate(array.shape)]
    main_axis = array.shape.index(max(array.shape))
    neighbour = place[:main_axis] + [(place[main_axis] + 1) % array.shape[main_axis]] + place[main_axis + 1:]
    return array.at[tuple(place)].set(least).at[tuple(neighbour)].set(high)


def block_scale(stream_key, shape, pieces, least, high):
    gain = 1.0
    for position, parts in pieces:
        steps = jax.random.uniform(jax.random.fold_in(jax.random.fold_in(stream_key, 6), position), (parts,), jnp.float32, least / len(pieces), high / len(pieces))
        gain = gain * jnp.repeat(jnp.exp(steps), shape[position] // parts).reshape((-1,) + (1,) * (len(shape) - 1 - position))
    return gain


def gaussian(stream_key, dims, scale, limit, cuts=(), kind=jnp.bfloat16):
    entries = scale * jax.random.normal(stream_key, dims, jnp.float32)
    if cuts:
        entries = entries * block_scale(stream_key, dims, cuts, -0.22, 0.18)
    return jnp.clip(entries, -limit, limit).astype(kind)


def setup_inputs(seed: int = 0) -> dict:
    seeds = jax.random.split(jax.random.key(seed), 8)
    return {
        "candidates": gaussian(seeds[0], (USERS, CANDS, D), 1.0, 6.0, ((0, 4), (1, 64))),
        "behav_keys": draw_behav_keys(jax.random.fold_in(seeds[7], 71), 0),
        "behav_values": draw_behav_values(jax.random.fold_in(seeds[7], 71), 0),
        "w_query": gaussian(seeds[3], (D, D), D ** -0.5, 0.5),
        "w_hidden": gaussian(seeds[4], (2 * D, HID), (2 * D) ** -0.5, 0.375),
        "w_out": gaussian(seeds[5], (HID,), HID ** -0.5, 0.1875, (), jnp.float32),
        "clicks": with_ends((jax.random.randint(seeds[6], (USERS, CANDS), 0, 2) < 1).astype(jnp.int32), jax.random.fold_in(seeds[6], 1), 0, 1),
    }


def attend_one(operands):
    query_rows, key_rows, value_rows = operands
    scale_factor = 1.0 / (HEAD ** 0.5)
    query_heads = query_rows.reshape(CANDS, HEADS, HEAD).astype(jnp.float32)
    key_heads = key_rows.reshape(N_SEQ, L_DEV, HEADS, HEAD).astype(jnp.float32)
    value_heads = value_rows.reshape(N_SEQ, L_DEV, HEADS, HEAD).astype(jnp.float32)
    scores = jnp.einsum("che,blhe->hcbl", query_heads, key_heads) * scale_factor
    block_max = jnp.max(scores, axis=-1)
    top = jnp.max(block_max, axis=-1)
    expos = jnp.exp(scores - block_max[..., None])
    probs = expos.astype(jnp.bfloat16).astype(jnp.float32)
    weights = jnp.exp(block_max - top[..., None])
    partial_num = jnp.einsum("hcbl,blhe->hcbe", probs, value_heads)
    numer = jnp.sum(partial_num * weights[..., None], axis=2)
    denom = jnp.sum(jnp.sum(expos, axis=-1) * weights, axis=-1)
    attended = numer / denom[..., None]
    return jnp.transpose(attended, (1, 0, 2)).reshape(CANDS, D).astype(jnp.bfloat16)


def reference(candidates, behav_keys, behav_values, w_query, w_hidden, w_out, clicks):
    queries = jnp.dot(candidates.reshape(-1, D), w_query, preferred_element_type=jnp.float32)
    queries = queries.astype(jnp.bfloat16).reshape(USERS, CANDS, D)
    attended = lax.map(attend_one, (queries, behav_keys, behav_values))
    features = jnp.concatenate([candidates, attended], axis=-1).reshape(-1, 2 * D)
    pre = jnp.dot(features, w_hidden, preferred_element_type=jnp.float32)
    hidden = jnp.maximum(pre, 0.0).astype(jnp.bfloat16)
    hidden_wide = hidden.astype(jnp.float32)
    logits = jnp.dot(hidden_wide, w_out, precision=lax.Precision.HIGHEST)
    dlogit = jax.nn.sigmoid(logits) - clicks.reshape(-1).astype(jnp.float32)
    grad_out = jnp.sum(hidden_wide * dlogit[:, None], axis=0)
    dpre = jnp.where(pre > 0.0, dlogit[:, None] * w_out[None, :], 0.0).astype(jnp.bfloat16)
    grad_hidden = lax.dot_general(features, dpre, (((0,), (0,)), ((), ())), preferred_element_type=jnp.float32)
    return logits.reshape(USERS, CANDS), grad_hidden, grad_out
```

```python
import functools
import math

import jax
import jax.numpy as jnp
from jax import lax
from jax.experimental import pallas as pl
from jax.experimental.pallas import tpu as pltpu
from jax.sharding import PartitionSpec as P

HEADS = 4
MESH = pl.DeviceIdType.MESH
NT = (((1,), (1,)), ((), ()))
F32 = jnp.float32
BF16 = jnp.bfloat16


def kernel(
    ns,
    ng,
    cand_hbm,
    keys_hbm,
    vals_hbm,
    wq_hbm,
    wh_hbm,
    wout_ref,
    clicks_ref,
    logits_ref,
    gh_ref,
    go_ref,
    x_buf,
    xf,
    qf,
    k_buf,
    v_buf,
    wq_buf,
    wh_buf,
    clk,
    a_send,
    a_recv,
    g_send,
    g_recv,
    z_buf,
    ga_buf,
    l_send,
    l_recv,
    o1,
    o2,
    o3,
    kv_sems,
    w_sems,
    send_sems,
    recv_sems,
):
    me = lax.axis_index("seq")
    grp = lax.axis_index("grp")
    users = k_buf.shape[0]
    length, width = k_buf.shape[1], k_buf.shape[2]
    per_dev = 2
    rows = users * per_dev
    parts = ns // users
    half = ns // 2
    u_me = me // parts
    q_me = lax.rem(me, parts)
    head_size = width // HEADS
    scale = math.log2(math.e) / math.sqrt(head_size)

    def peer(k):
        return lax.rem(me + k, ns)

    def remote(src, dst, phase, seq, group=None):
        where = {"seq": seq} if group is None else {"seq": seq, "grp": group}
        return pltpu.make_async_remote_copy(
            src_ref=src,
            dst_ref=dst,
            send_sem=send_sems.at[phase],
            recv_sem=recv_sems.at[phase],
            device_id=where,
            device_id_type=MESH,
        )

    def local(src, dst, sem):
        return pltpu.make_async_copy(src, dst, sem)

    def wait_send(ref, phase):
        local(ref, ref, send_sems.at[phase]).wait()

    def wait_recv(ref, phase):
        local(ref, ref, recv_sems.at[phase]).wait()

    own_load = local(cand_hbm, x_buf.at[me], w_sems.at[0])
    own_load.start()
    wq_load = local(wq_hbm, wq_buf, w_sems.at[1])
    wq_load.start()

    @pl.loop(0, users)
    def _(t):
        u = lax.rem(u_me + 1 + t, users)
        local(keys_hbm.at[u], k_buf.at[u], kv_sems.at[0, t]).start()
        local(vals_hbm.at[u], v_buf.at[u], kv_sems.at[1, t]).start()

    wh_load = local(wh_hbm, wh_buf, w_sems.at[2])
    wh_load.start()

    barrier = pltpu.get_barrier_semaphore()

    @pl.loop(1, ns)
    def _(k):
        pl.semaphore_signal(barrier, inc=1, device_id={"seq": peer(k)}, device_id_type=MESH)

    for k in range(1, ng):
        pl.semaphore_signal(
            barrier,
            inc=1,
            device_id={"seq": me, "grp": lax.rem(grp + k, ng)},
            device_id_type=MESH,
        )
    pl.semaphore_wait(barrier, ns - 1 + ng - 1)

    own_load.wait()

    @pl.loop(1, ns)
    def _(k):
        remote(x_buf.at[me], x_buf.at[me], 0, peer(k)).start()

    clicks_wide = clicks_ref[...].astype(F32)
    for c in range(per_dev):
        clk[c] = jnp.broadcast_to(clicks_wide[:, c : c + 1], (users, width))

    wq_load.wait()
    wait_recv(x_buf.at[pl.ds(0, ns - 1)], 0)
    x_all = x_buf[...].reshape(ns * rows, width)
    xf[...] = x_all.astype(F32)
    qf[...] = (
        jnp.dot(x_all, wq_buf[...], preferred_element_type=F32).astype(BF16).astype(F32)
    )

    lane = lax.broadcasted_iota(jnp.int32, (ns * per_dev, width), 1)
    head_of = lane // head_size
    lane8 = lax.broadcasted_iota(jnp.int32, (8, width), 1)
    row8 = lax.broadcasted_iota(jnp.int32, (8, width), 0)
    group8 = lax.rem(lane8, head_size) // 8
    is_lse = lax.rem(lane8, 8) == 0
    is_click = lax.rem(lane8, 8) == 1
    my_half = me // half
    my_place = lax.rem(me, half)
    at_me = (row8 == lax.rem(my_place, 8)) & (group8 == my_place // 8) & is_click

    @pl.loop(0, users)
    def _(t):
        u = lax.rem(u_me + 1 + t, users)
        local(keys_hbm.at[u], k_buf.at[u], kv_sems.at[0, t]).wait()
        local(vals_hbm.at[u], v_buf.at[u], kv_sems.at[1, t]).wait()
        queries = jnp.concatenate(
            [qf[pl.ds(u * per_dev + c, ns, stride=rows), :] for c in range(per_dev)], axis=0
        )
        keys = k_buf[u]
        vals = v_buf[u]
        att = jnp.zeros((ns * per_dev, width), F32)
        lse = jnp.zeros((ns * per_dev, width), F32)
        for h in range(HEADS):
            qh = jnp.where(head_of == h, queries, 0.0).astype(BF16)
            s = lax.dot_general(qh, keys, NT, preferred_element_type=F32)
            m = jnp.max(s, axis=-1, keepdims=True)
            p = jnp.exp2((s - m) * scale)
            den = jnp.sum(p, axis=-1, keepdims=True)
            o = jnp.dot(p.astype(BF16), vals, preferred_element_type=F32)
            att = att + jnp.where(head_of == h, o * (1.0 / den), 0.0)
            lse = lse + jnp.where(head_of == h, m * scale + jnp.log2(den), 0.0)
        for q in range(parts):
            slot = u * parts + q
            step = ns * per_dev // parts
            a_send[slot, 0:32] = att[step * q : step * q + 32]
            tile = jnp.zeros((8, width), F32)
            for g in range(4):
                first = step * q + 8 * g
                tile = jnp.where(is_lse & (group8 == g), lse[first : first + 8], tile)
            click = jnp.broadcast_to(clk[q // 2, pl.ds(u, 1), :], (8, width))
            shown = jnp.where(my_half == q % 2, 1.0, 0.0)
            a_send[slot, 32:40] = jnp.where(at_me, click * shown, tile)

            @pl.when(slot != me)
            def _():
                remote(a_send.at[slot], a_recv.at[me], 1, slot).start()

            @pl.when(slot == me)
            def _():
                local(a_send.at[slot], a_recv.at[me], recv_sems.at[1]).start()

    wait_send(x_buf.at[pl.ds(0, ns - 1)], 0)
    wait_recv(a_recv, 1)

    ej = lax.broadcasted_iota(jnp.int32, (width, 4 * width), 0)
    ef = lax.broadcasted_iota(jnp.int32, (width, 4 * width), 1)
    same = (ej // head_size == lax.rem(ef, width) // head_size) & (
        lax.rem(ej, head_size) // 8 == ef // width
    )
    spread = jnp.where(same & (lax.rem(ej, 8) == 0), 1.0, 0.0).astype(BF16)
    spread_click = jnp.where(same & (lax.rem(ej, 8) == 1), 1.0, 0.0).astype(BF16)
    tiles = a_recv[:, 32:40, :]
    rest = tiles.reshape(ns * 8, width)
    lse_all = jnp.zeros((ns * 8, 4 * width), F32)
    for _ in range(3):
        piece = rest.astype(BF16)
        rest = rest - piece.astype(F32)
        lse_all = lse_all + jnp.dot(piece, spread, preferred_element_type=F32)
    lse_all = lse_all.reshape(ns, 8, 4 * width)
    top = jnp.max(lse_all, axis=0)
    w = jnp.exp2(lse_all - top[None])
    den = jnp.sum(w, axis=0)
    attended = []
    for g in range(4):
        cols = slice(g * width, g * width + width)
        num = jnp.sum(a_recv[:, 8 * g : 8 * g + 8, :] * w[:, :, cols], axis=0)
        attended.append(num / den[:, cols])
    attended = jnp.concatenate(attended, axis=0)
    click_tile = jnp.where(is_click, jnp.sum(tiles, axis=0), 0.0)
    click = jnp.dot(click_tile.astype(BF16), spread_click, preferred_element_type=F32)
    click = jnp.concatenate([click[:, g * width : g * width + width] for g in range(4)], axis=0)
    click = click[:, 0:1]

    first = half * lax.rem(q_me, 2) * rows + u_me * per_dev + q_me // 2
    cand = xf[pl.ds(first, 32, stride=rows), :]
    features = jnp.concatenate([cand, attended.astype(BF16).astype(F32)], axis=1)
    wh_load.wait()
    pre = jnp.dot(features.astype(BF16), wh_buf[...], preferred_element_type=F32)
    hidden = jnp.maximum(pre, 0.0).astype(BF16).astype(F32)
    wout = wout_ref[...]
    logits = jnp.sum(hidden * wout, axis=-1, keepdims=True)
    dlogit = 1.0 / (1.0 + jnp.exp(-logits)) - click
    dpre = jnp.where(pre > 0.0, dlogit * wout, 0.0).astype(BF16)
    grad = jnp.dot(
        jnp.transpose(features).astype(BF16), dpre, preferred_element_type=F32
    )
    cols = 4
    bw = grad.shape[1] // cols
    for b in range(ns):
        i, j = b // cols, b % cols
        g_send[b] = grad[16 * i : 16 * i + 16, bw * j : bw * j + bw].astype(BF16)

    @pl.loop(1, ns)
    def _(k):
        p = peer(k)
        remote(g_send.at[p], g_recv.at[me], 2, p).start()

    g_recv[me] = g_send[me]

    lo, hi8 = lax.rem(me, 8), me // 8
    out_part = jnp.sum(hidden * dlogit, axis=0, keepdims=True)
    for i in range(8):
        o1[lo, i : i + 1, :] = out_part[:, width * i : width * i + width]
    for k in range(1, 8):
        remote(o1.at[lo], o1.at[lo], 3, hi8 * 8 + lax.rem(lo + k, 8)).start()

    wide = jnp.broadcast_to(logits, (32, width))
    for i in range(32):
        l_send[i] = wide[i : i + 1, :]
    l_slot = (q_me // 2) * users + u_me

    @pl.loop(0, 32)
    def _(i):
        d = half * lax.rem(q_me, 2) + i

        @pl.when(d != me)
        def _():
            remote(l_send.at[i], l_recv.at[l_slot], 4, d).start()

        @pl.when(d == me)
        def _():
            local(l_send.at[i], l_recv.at[l_slot], recv_sems.at[4]).start()

    wait_recv(o1.at[pl.ds(0, 7)], 3)
    o2[grp] = jnp.sum(o1[...], axis=0)
    for k in range(1, ng):
        remote(o2.at[grp], o2.at[grp], 5, me, lax.rem(grp + k, ng)).start()
    wait_recv(g_recv.at[pl.ds(0, ns - 1)], 2)
    z_buf[grp] = jnp.sum(g_recv[...].astype(F32), axis=0)
    for k in range(1, ng):
        remote(z_buf.at[grp], z_buf.at[grp], 6, me, lax.rem(grp + k, ng)).start()
    wait_recv(o2.at[pl.ds(0, ng - 1)], 5)
    o3[hi8] = jnp.sum(o2[...], axis=0)
    for k in range(1, 8):
        remote(o3.at[hi8], o3.at[hi8], 7, lax.rem(hi8 + k, 8) * 8 + lo).start()
    wait_recv(z_buf.at[pl.ds(0, ng - 1)], 6)
    ga_buf[me] = jnp.sum(z_buf[...], axis=0).astype(BF16)

    @pl.loop(1, ns)
    def _(k):
        remote(ga_buf.at[me], ga_buf.at[me], 8, peer(k)).start()

    wait_recv(l_recv, 4)
    logit_rows = l_recv[...].reshape(2 * users, width)
    lane_u = lax.broadcasted_iota(jnp.int32, (users, width), 1)
    logits_ref[...] = jnp.where(lane_u == 0, logit_rows[:users], logit_rows[users:])
    wait_recv(o3.at[pl.ds(0, 7)], 7)
    go_ref[...] = jnp.sum(o3[...], axis=0)
    wait_recv(ga_buf.at[pl.ds(0, ns - 1)], 8)
    for b in range(ns):
        i, j = b // cols, b % cols
        gh_ref[16 * i : 16 * i + 16, bw * j : bw * j + bw] = ga_buf[b].astype(F32)

    @pl.loop(0, users)
    def _(t):
        u = lax.rem(u_me + 1 + t, users)
        for q in range(parts):

            @pl.when(u * parts + q != me)
            def _():
                wait_send(a_send.at[0], 1)

    wait_send(g_send.at[pl.ds(0, ns - 1)], 2)
    wait_send(o1.at[pl.ds(0, 7)], 3)

    @pl.loop(0, 32)
    def _(i):
        @pl.when(half * lax.rem(q_me, 2) + i != me)
        def _():
            wait_send(l_send.at[0], 4)

    wait_send(o2.at[pl.ds(0, ng - 1)], 5)
    wait_send(z_buf.at[pl.ds(0, ng - 1)], 6)
    wait_send(o3.at[pl.ds(0, 7)], 7)
    wait_send(ga_buf.at[pl.ds(0, ns - 1)], 8)


def on_device(ns, ng, candidates, behav_keys, behav_values, w_query, w_hidden, w_out, clicks):
    users, per_dev, width = candidates.shape
    length = behav_keys.shape[1]
    feats, hid = w_hidden.shape
    rows = users * per_dev
    any_spec = pl.BlockSpec(memory_space=pl.ANY)
    vmem_spec = pl.BlockSpec(memory_space=pltpu.VMEM)
    logits, grad_hidden, grad_out = pl.pallas_call(
        functools.partial(kernel, ns, ng),
        out_shape=(
            jax.ShapeDtypeStruct((users, width), F32),
            jax.ShapeDtypeStruct((feats, hid), F32),
            jax.ShapeDtypeStruct((8, hid // 8), F32),
        ),
        in_specs=[any_spec] * 5 + [vmem_spec] * 2,
        out_specs=(vmem_spec, vmem_spec, vmem_spec),
        scratch_shapes=[
            pltpu.VMEM((ns, rows, width), BF16),
            pltpu.VMEM((ns * rows, width), F32),
            pltpu.VMEM((ns * rows, width), F32),
            pltpu.VMEM((users, length, width), BF16),
            pltpu.VMEM((users, length, width), BF16),
            pltpu.VMEM((width, width), BF16),
            pltpu.VMEM((feats, hid), BF16),
            pltpu.VMEM((per_dev, users, width), F32),
            pltpu.VMEM((ns, 40, width), F32),
            pltpu.VMEM((ns, 40, width), F32),
            pltpu.VMEM((ns, 16, hid // 4), BF16),
            pltpu.VMEM((ns, 16, hid // 4), BF16),
            pltpu.VMEM((ng, 16, hid // 4), F32),
            pltpu.VMEM((ns, 16, hid // 4), BF16),
            pltpu.VMEM((32, 1, width), F32),
            pltpu.VMEM((32, 1, width), F32),
            pltpu.VMEM((8, 8, hid // 8), F32),
            pltpu.VMEM((ng, 8, hid // 8), F32),
            pltpu.VMEM((8, 8, hid // 8), F32),
            pltpu.SemaphoreType.DMA((2, users)),
            pltpu.SemaphoreType.DMA((3,)),
            pltpu.SemaphoreType.DMA((9,)),
            pltpu.SemaphoreType.DMA((9,)),
        ],
        compiler_params=pltpu.CompilerParams(
            collective_id=0, has_side_effects=True, vmem_limit_bytes=50 * 2**20
        ),
        name="ranker",
    )(
        candidates.reshape(rows, width),
        behav_keys,
        behav_values,
        w_query,
        w_hidden,
        w_out.reshape(1, hid),
        clicks,
    )
    return logits[:, :per_dev], grad_hidden, grad_out.reshape(hid)


def solution(mesh):
    return jax.shard_map(
        functools.partial(on_device, mesh.shape["seq"], mesh.shape["grp"]),
        mesh=mesh,
        in_specs=(
            P("grp", "seq", None),
            P("grp", "seq", None),
            P("grp", "seq", None),
            P(),
            P(),
            P(),
            P("grp", "seq"),
        ),
        out_specs=(P("grp", "seq"), P(), P()),
        check_vma=False,
    )
```

```python
import functools
import math

import jax
import jax.numpy as jnp
from jax import lax
from jax.experimental import pallas as pl
from jax.experimental.pallas import tpu as pltpu
from jax.sharding import PartitionSpec as P

HEADS = 4
MESH = pl.DeviceIdType.MESH
NT = (((1,), (1,)), ((), ()))
F32 = jnp.float32
BF16 = jnp.bfloat16
GATHER, GATHER_TWIN, PARTIAL, TWIN_HEAD, REDUCE, OUT_X, LOGITS, OUT_GRP, GRP, OUT_ZY, ALL, ALL_TWIN, OUT_TWIN = (
    0, 2, 4, 5, 6, 7, 8, 9, 10, 11, 12, 13, 14
)
PHASES = 15
CHUNK = 512


def kernel(
    nc,
    ng,
    cand_hbm,
    keys_hbm,
    vals_hbm,
    wq_hbm,
    wh_hbm,
    wout_ref,
    clicks_ref,
    logits_ref,
    gh_ref,
    go_ref,
    x_buf,
    xf,
    qf,
    k_buf,
    v_buf,
    s_even,
    s_odd,
    q_heads,
    wq_buf,
    wh_buf,
    clk,
    mine,
    theirs,
    p_send,
    p_recv,
    h_send,
    h_recv,
    g_send,
    g_recv,
    z_buf,
    ga_buf,
    l_send,
    l_recv,
    o1,
    o2,
    o3,
    o4,
    kv_sems,
    w_sems,
    twin_sems,
    twin_send_sem,
    send_sems,
    recv_sems,
):
    me = lax.axis_index("seq")
    grp = lax.axis_index("grp")
    core = lax.rem(me, 2)
    chip = me // 2
    users, length, width = k_buf.shape
    half_users = users // 2
    u_me = me // 4
    c_me = lax.rem(chip, 2)
    first_half = u_me // half_users
    head_size = width // HEADS
    scale = math.log2(math.e) / math.sqrt(head_size)
    hw = HEADS * width

    def user_at(t):
        return lax.rem(first_half + t // half_users, 2) * half_users + lax.rem(
            u_me + 1 + t, half_users
        )

    def on_chip(k):
        return lax.rem(chip + k, nc)

    def remote(src, dst, phase, seq, group=None):
        where = {"seq": seq} if group is None else {"seq": seq, "grp": group}
        return pltpu.make_async_remote_copy(
            src_ref=src,
            dst_ref=dst,
            send_sem=send_sems.at[phase],
            recv_sem=recv_sems.at[phase],
            device_id=where,
            device_id_type=MESH,
        )

    twin = chip * 2 + 1 - core

    def same_core(other_chip):
        return other_chip * 2 + core

    def local(src, dst, sem):
        return pltpu.make_async_copy(src, dst, sem)

    def wait_send(ref, phase):
        local(ref, ref, send_sems.at[phase]).wait()

    def wait_recv(ref, phase):
        local(ref, ref, recv_sems.at[phase]).wait()

    own_loads = [
        local(cand_hbm.at[pl.ds(16 * i, 16)], x_buf.at[i, core * nc + chip], w_sems.at[i])
        for i in range(2)
    ]
    for load in own_loads:
        load.start()
    wq_load = local(wq_hbm, wq_buf, w_sems.at[2])
    wq_load.start()

    @pl.loop(0, users)
    def _(t):
        u = user_at(t)
        local(keys_hbm.at[u], k_buf.at[u], kv_sems.at[0, t]).start()
        local(vals_hbm.at[u], v_buf.at[u], kv_sems.at[1, t]).start()

    wh_load = local(wh_hbm, wh_buf, w_sems.at[3])
    wh_load.start()

    barrier = pltpu.get_barrier_semaphore()
    pl.semaphore_signal(barrier, inc=1, device_id={"seq": twin}, device_id_type=MESH)

    @pl.loop(1, nc)
    def _(k):
        pl.semaphore_signal(
            barrier, inc=1, device_id={"seq": same_core(on_chip(k))}, device_id_type=MESH
        )

    for k in range(1, ng):
        pl.semaphore_signal(
            barrier,
            inc=1,
            device_id={"seq": me, "grp": lax.rem(grp + k, ng)},
            device_id_type=MESH,
        )

    row_u = lax.broadcasted_iota(jnp.int32, (users, users), 0)
    col_u = lax.broadcasted_iota(jnp.int32, (users, users), 1)
    for c in range(2):
        wide = jnp.broadcast_to(clicks_ref[c : c + 1, :].astype(F32), (users, users))
        column = jnp.sum(jnp.where(row_u == col_u, wide, 0.0), axis=1, keepdims=True)
        clk[c] = jnp.broadcast_to(column, (users, width))

    pl.semaphore_wait(barrier, nc + ng - 1)

    for load in own_loads:
        load.wait()
    own = core * nc + chip
    for turn in range(2):

        @pl.loop(1, nc)
        def _(k):
            to = on_chip(k)
            part = lax.rem(to // (nc // 2) + turn, 2)
            remote(
                x_buf.at[part, own], x_buf.at[part, own], GATHER + part, same_core(to)
            ).start()

    def pass_on(part):
        wait_recv(x_buf.at[0, pl.ds(0, nc - 1)], GATHER + part)
        block = x_buf.at[part, pl.ds(core * nc, nc)]
        remote(block, block, GATHER_TWIN + part, twin).start()

    def make_queries(part):
        wait_recv(x_buf.at[0, pl.ds(0, nc)], GATHER_TWIN + part)
        x_all = x_buf[part].reshape(2 * nc * 16, width)
        xf[part] = x_all.astype(F32)
        queries = jnp.dot(x_all, wq_buf[...], preferred_element_type=F32)
        qf[part] = queries.astype(BF16).astype(F32)

    second_half = 1 - first_half
    wq_load.wait()
    pass_on(first_half)
    make_queries(first_half)

    head_of = lax.broadcasted_iota(jnp.int32, (2 * nc, width), 1) // head_size
    lane8 = lax.broadcasted_iota(jnp.int32, (8, width), 1)
    row8 = lax.broadcasted_iota(jnp.int32, (8, width), 0)
    group8 = lax.rem(lane8, head_size) // 8
    is_lse = lax.rem(lane8, 8) == 0
    is_click = lax.rem(lane8, 8) == 1
    at_me = (row8 == lax.rem(chip, 8)) & (group8 == chip // 8) & is_click

    def set_queries(u):
        part = u // half_users
        for c in range(2):
            rows = qf[part, pl.ds(lax.rem(u, half_users) * 2 + c, 2 * nc, stride=16), :]
            for h in range(HEADS):
                first = h * width + c * 2 * nc
                q_heads[first : first + 2 * nc, :] = jnp.where(head_of == h, rows, 0.0).astype(
                    BF16
                )

    def scores(u, j, s_ref, highest):
        rows = slice(j * CHUNK, j * CHUNK + CHUNK)
        s = lax.dot_general(k_buf[u, rows, :], q_heads[...], NT, preferred_element_type=F32)
        s_ref[rows, :] = s
        return jnp.maximum(highest, jnp.max(s.reshape(CHUNK // 8, 8, hw), axis=0))

    lowest = jnp.full((8, hw), -jnp.inf, F32)

    def attend(t, s_ref, s_next, highest):
        u = user_at(t)
        top = jnp.max(highest, axis=0, keepdims=True) * scale
        local(vals_hbm.at[u], v_buf.at[u], kv_sems.at[1, t]).wait()
        vals = jnp.transpose(v_buf[u])
        t_next = jnp.minimum(t + 1, users - 1)
        u_next = user_at(t_next)

        @pl.when(t + 1 < users)
        def _():
            local(keys_hbm.at[u_next], k_buf.at[u_next], kv_sems.at[0, t_next]).wait()

        set_queries(u_next)
        highest = lowest
        den = jnp.zeros((8, hw), F32)
        num = [jnp.zeros((2 * head_size, 2 * width), F32) for _ in range(HEADS // 2)]
        for j in range(length // CHUNK):
            highest = scores(u_next, j, s_next, highest)
            rows = slice(j * CHUNK, j * CHUNK + CHUNK)
            p = jnp.exp2(s_ref[rows, :] * scale - top)
            den = den + jnp.sum(p.reshape(CHUNK // 8, 8, hw), axis=0)
            probs = p.astype(BF16)
            for h in range(HEADS // 2):
                num[h] = num[h] + jnp.dot(
                    vals[2 * head_size * h : 2 * head_size * (h + 1), rows],
                    probs[:, 2 * width * h : 2 * width * (h + 1)],
                    preferred_element_type=F32,
                )
        den = jnp.sum(den, axis=0, keepdims=True)
        inverse = 1.0 / den
        lse = top + jnp.log2(den)
        att_rows, lse_rows = [], []
        for h in range(HEADS):
            cols = slice(width * h, width * (h + 1))
            sub, at = head_size * (h % 2), width * (h % 2)
            block = num[h // 2][sub : sub + head_size, at : at + width]
            att_rows.append(block * inverse[:, cols])
            lse_rows.append(jnp.broadcast_to(lse[:, cols], (head_size, width)))
        att = jnp.transpose(jnp.concatenate(att_rows, axis=0))
        lse = jnp.transpose(jnp.concatenate(lse_rows, axis=0))
        for c in range(2):
            for half in range(2):
                first = 64 * c + 32 * half
                mine[t, half, c, 0:32] = att[first : first + 32]
                mine[t, half, c, 32:64] = lse[first : first + 32]
        pltpu.make_async_remote_copy(
            src_ref=mine.at[t, 1 - core],
            dst_ref=theirs.at[t],
            send_sem=twin_send_sem,
            recv_sem=twin_sems.at[t],
            device_id={"seq": twin},
            device_id_type=MESH,
        ).start()
        return highest

    def merge(t):
        u = user_at(t)
        local(theirs.at[t], theirs.at[t], twin_sems.at[t]).wait()
        for c in range(2):
            a, b = mine[t, core, c], theirs[t, c]
            top = jnp.maximum(a[32:64], b[32:64])
            wa, wb = jnp.exp2(a[32:64] - top), jnp.exp2(b[32:64] - top)
            total = wa + wb
            lse = top + jnp.log2(total)
            slot = t * 2 + c
            p_send[slot, 0:32] = (a[0:32] * wa + b[0:32] * wb) / total
            tile = jnp.zeros((8, width), F32)
            for g in range(4):
                tile = jnp.where(is_lse & (group8 == g), lse[8 * g : 8 * g + 8], tile)
            click = jnp.broadcast_to(clk[c, pl.ds(u, 1), :], (8, width))
            p_send[slot, 32:40] = jnp.where(at_me, click, tile)
            to = 4 * u + 2 * c + core

            @pl.when(to != me)
            def _():
                remote(p_send.at[slot], p_recv.at[chip], PARTIAL, to).start()

            @pl.when(to == me)
            def _():
                local(p_send.at[slot], p_recv.at[chip], recv_sems.at[PARTIAL]).start()

    u_first = user_at(0)
    local(keys_hbm.at[u_first], k_buf.at[u_first], kv_sems.at[0, 0]).wait()
    set_queries(u_first)
    highest = lowest
    for j in range(length // CHUNK):
        highest = scores(u_first, j, s_even, highest)

    def two_users(i, highest):
        t = 2 * i

        @pl.when(i == 1)
        def _():
            pass_on(second_half)

        highest = attend(t, s_even, s_odd, highest)

        @pl.when(i > 0)
        def _():
            merge(t - 1)

        @pl.when(i == half_users // 2 - 1)
        def _():
            make_queries(second_half)

        highest = attend(t + 1, s_odd, s_even, highest)
        merge(t)
        return highest

    lax.fori_loop(0, users // 2, two_users, highest)
    merge(users - 1)

    wait_recv(p_recv, PARTIAL)
    ej = lax.broadcasted_iota(jnp.int32, (width, 4 * width), 0)
    ef = lax.broadcasted_iota(jnp.int32, (width, 4 * width), 1)
    same = (ej // head_size == lax.rem(ef, width) // head_size) & (
        lax.rem(ej, head_size) // 8 == ef // width
    )
    spread = jnp.where(same & (lax.rem(ej, 8) == 0), 1.0, 0.0).astype(BF16)
    spread_click = jnp.where(same & (lax.rem(ej, 8) == 1), 1.0, 0.0).astype(BF16)
    tiles = p_recv[:, 32:40, :]
    rest = tiles.reshape(nc * 8, width)
    lse_all = jnp.zeros((nc * 8, 4 * width), F32)
    for _ in range(3):
        piece = rest.astype(BF16)
        rest = rest - piece.astype(F32)
        lse_all = lse_all + jnp.dot(piece, spread, preferred_element_type=F32)
    lse_all = lse_all.reshape(nc, 8, 4 * width)
    w = jnp.exp2(lse_all - jnp.max(lse_all, axis=0)[None])
    den = jnp.sum(w, axis=0)
    attended = []
    for g in range(4):
        cols = slice(g * width, g * width + width)
        num = jnp.sum(p_recv[:, 8 * g : 8 * g + 8, :] * w[:, :, cols], axis=0)
        attended.append(num / den[:, cols])
    attended = jnp.concatenate(attended, axis=0).astype(BF16).astype(F32)
    click_tile = jnp.where(is_click, jnp.sum(tiles, axis=0), 0.0)
    click = jnp.dot(click_tile.astype(BF16), spread_click, preferred_element_type=F32)
    click = jnp.concatenate([click[:, g * width : g * width + width] for g in range(4)], axis=0)
    click = click[:, 0:1]

    def candidates_of(which):
        first = which * nc * 16 + lax.rem(u_me, half_users) * 2 + c_me
        return xf[first_half, pl.ds(first, nc, stride=16), :]

    features = jnp.concatenate([candidates_of(core), attended], axis=1)
    wh_load.wait()
    pre = jnp.dot(features.astype(BF16), wh_buf[...], preferred_element_type=F32)
    hidden = jnp.maximum(pre, 0.0).astype(BF16).astype(F32)
    logits = jnp.sum(hidden * wout_ref[...], axis=-1, keepdims=True)
    dlogit = 1.0 / (1.0 + jnp.exp(-logits)) - click
    h_send[0:32] = attended
    h_send[32:64] = jnp.broadcast_to(dlogit, (nc, width))
    remote(h_send, h_recv, TWIN_HEAD, twin).start()

    wide = jnp.broadcast_to(logits, (nc, width))
    for i in range(nc):
        l_send[i] = wide[i : i + 1, :]
    l_slot = c_me * users + u_me

    @pl.loop(1, nc)
    def _(k):
        to = on_chip(k)
        remote(l_send.at[to], l_recv.at[l_slot], LOGITS, same_core(to)).start()

    l_recv[l_slot] = l_send[chip]

    half_hid = wh_buf.shape[1] // 2
    my_cols = pl.ds(pl.multiple_of(core * half_hid, half_hid), half_hid)
    wout = wout_ref[:, my_cols]
    wait_recv(h_recv, TWIN_HEAD)
    other = jnp.concatenate([candidates_of(1 - core), h_recv[0:32]], axis=1)
    features = jnp.concatenate([features, other], axis=0)
    dlogit = jnp.concatenate([dlogit, h_recv[32:64, 0:1]], axis=0)
    pre = jnp.dot(features.astype(BF16), wh_buf[:, my_cols], preferred_element_type=F32)
    hidden = jnp.maximum(pre, 0.0).astype(BF16).astype(F32)
    dpre = jnp.where(pre > 0.0, dlogit * wout, 0.0).astype(BF16)
    grad = jnp.dot(jnp.transpose(features).astype(BF16), dpre, preferred_element_type=F32)
    bw = half_hid // 2
    for b in range(nc):
        i, j = b // 2, b % 2
        g_send[b] = grad[16 * i : 16 * i + 16, bw * j : bw * j + bw].astype(BF16)

    @pl.loop(1, nc)
    def _(k):
        to = on_chip(k)
        remote(g_send.at[to], g_recv.at[chip], REDUCE, same_core(to)).start()

    g_recv[chip] = g_send[chip]

    at_x, at_zy = lax.rem(chip, 4), chip // 4
    out_part = jnp.sum(hidden * dlogit, axis=0, keepdims=True)
    pieces = [out_part[:, width * i : width * i + width] for i in range(4)]
    o1[at_x] = jnp.concatenate(pieces + [jnp.zeros((4, width), F32)], axis=0)
    for k in range(1, 4):
        to = at_zy * 4 + lax.rem(at_x + k, 4)
        remote(o1.at[at_x], o1.at[at_x], OUT_X, same_core(to)).start()

    wait_recv(o1.at[pl.ds(0, 3)], OUT_X)
    o2[grp] = o1[0] + o1[1] + o1[2] + o1[3]
    for k in range(1, ng):
        remote(o2.at[grp], o2.at[grp], OUT_GRP, me, lax.rem(grp + k, ng)).start()
    wait_recv(g_recv.at[pl.ds(0, nc - 1)], REDUCE)
    z_buf[grp] = jnp.sum(g_recv[...].astype(F32), axis=0)
    for k in range(1, ng):
        remote(z_buf.at[grp], z_buf.at[grp], GRP, me, lax.rem(grp + k, ng)).start()
    wait_recv(o2.at[pl.ds(0, ng - 1)], OUT_GRP)
    o3[at_zy] = jnp.sum(o2[...], axis=0)
    for k in range(1, 8):
        to = lax.rem(at_zy + k, 8) * 4 + at_x
        remote(o3.at[at_zy], o3.at[at_zy], OUT_ZY, same_core(to)).start()
    wait_recv(z_buf.at[pl.ds(0, ng - 1)], GRP)
    ga_buf[core, chip] = jnp.sum(z_buf[...], axis=0).astype(BF16)

    @pl.loop(1, nc)
    def _(k):
        block = ga_buf.at[core, chip]
        remote(block, block, ALL, same_core(on_chip(k))).start()

    wait_recv(l_recv.at[pl.ds(0, nc - 1)], LOGITS)
    logit_rows = l_recv[...].reshape(2 * users, width)
    row_o = lax.broadcasted_iota(jnp.int32, (users, width), 0)
    col_o = lax.broadcasted_iota(jnp.int32, (users, width), 1)
    for c in range(2):
        rows = jnp.where(row_o == col_o, logit_rows[users * c : users * (c + 1)], 0.0)
        logits_ref[c : c + 1, :] = jnp.sum(rows, axis=0, keepdims=True)[:, :users]
    wait_recv(o3.at[pl.ds(0, 7)], OUT_ZY)
    o4[core] = jnp.sum(o3[...], axis=0)
    remote(o4.at[core], o4.at[core], OUT_TWIN, twin).start()

    for part in range(2):
        wait_send(x_buf.at[0, pl.ds(0, nc - 1)], GATHER + part)
        wait_send(x_buf.at[0, pl.ds(0, nc)], GATHER_TWIN + part)
    local(theirs, theirs, twin_send_sem).wait()
    wait_send(p_send.at[pl.ds(0, nc - 1)], PARTIAL)
    wait_send(h_send, TWIN_HEAD)
    wait_send(l_send.at[pl.ds(0, nc - 1)], LOGITS)
    wait_send(g_send.at[pl.ds(0, nc - 1)], REDUCE)
    wait_send(o1.at[pl.ds(0, 3)], OUT_X)
    wait_send(o2.at[pl.ds(0, ng - 1)], OUT_GRP)
    wait_send(z_buf.at[pl.ds(0, ng - 1)], GRP)
    wait_send(o3.at[pl.ds(0, 7)], OUT_ZY)

    wait_recv(ga_buf.at[0, pl.ds(0, nc - 1)], ALL)
    remote(ga_buf.at[core], ga_buf.at[core], ALL_TWIN, twin).start()

    def write(side):
        for j in range(2):
            cols = pl.ds(pl.multiple_of(side * half_hid + j * bw, bw), bw)
            for i in range(nc // 2):
                gh_ref[16 * i : 16 * i + 16, cols] = ga_buf[side, 2 * i + j].astype(F32)

    write(core)
    wait_recv(o4.at[0], OUT_TWIN)
    go_ref[...] = jnp.concatenate([o4[0, 0:4], o4[1, 0:4]], axis=0)
    wait_recv(ga_buf.at[0], ALL_TWIN)
    write(1 - core)
    wait_send(ga_buf.at[0, pl.ds(0, nc - 1)], ALL)
    wait_send(ga_buf.at[0], ALL_TWIN)
    wait_send(o4.at[0], OUT_TWIN)


def on_device(ns, ng, candidates, behav_keys, behav_values, w_query, w_hidden, w_out, clicks):
    users, per_dev, width = candidates.shape
    length = behav_keys.shape[1]
    feats, hid = w_hidden.shape
    nc = ns // 2
    any_spec = pl.BlockSpec(memory_space=pl.ANY)
    vmem_spec = pl.BlockSpec(memory_space=pltpu.VMEM)
    logits, grad_hidden, grad_out = pl.pallas_call(
        functools.partial(kernel, nc, ng),
        out_shape=(
            jax.ShapeDtypeStruct((per_dev, users), F32),
            jax.ShapeDtypeStruct((feats, hid), F32),
            jax.ShapeDtypeStruct((8, width), F32),
        ),
        in_specs=[any_spec] * 5 + [vmem_spec] * 2,
        out_specs=(vmem_spec, vmem_spec, vmem_spec),
        scratch_shapes=[
            pltpu.VMEM((2, ns, 16, width), BF16),
            pltpu.VMEM((2, ns * 16, width), F32),
            pltpu.VMEM((2, ns * 16, width), F32),
            pltpu.VMEM((users, length, width), BF16),
            pltpu.VMEM((users, length, width), BF16),
            pltpu.VMEM((length, HEADS * width), F32),
            pltpu.VMEM((length, HEADS * width), F32),
            pltpu.VMEM((HEADS * width, width), BF16),
            pltpu.VMEM((width, width), BF16),
            pltpu.VMEM((feats, hid), BF16),
            pltpu.VMEM((per_dev, users, width), F32),
            pltpu.VMEM((users, 2, 2, 64, width), F32),
            pltpu.VMEM((users, 2, 64, width), F32),
            pltpu.VMEM((nc, 40, width), F32),
            pltpu.VMEM((nc, 40, width), F32),
            pltpu.VMEM((64, width), F32),
            pltpu.VMEM((64, width), F32),
            pltpu.VMEM((nc, 16, hid // 4), BF16),
            pltpu.VMEM((nc, 16, hid // 4), BF16),
            pltpu.VMEM((ng, 16, hid // 4), F32),
            pltpu.VMEM((2, nc, 16, hid // 4), BF16),
            pltpu.VMEM((nc, 1, width), F32),
            pltpu.VMEM((nc, 1, width), F32),
            pltpu.VMEM((4, 8, width), F32),
            pltpu.VMEM((ng, 8, width), F32),
            pltpu.VMEM((8, 8, width), F32),
            pltpu.VMEM((2, 8, width), F32),
            pltpu.SemaphoreType.DMA((2, users)),
            pltpu.SemaphoreType.DMA((4,)),
            pltpu.SemaphoreType.DMA((users,)),
            pltpu.SemaphoreType.DMA,
            pltpu.SemaphoreType.DMA((PHASES,)),
            pltpu.SemaphoreType.DMA((PHASES,)),
        ],
        compiler_params=pltpu.CompilerParams(
            collective_id=0, has_side_effects=True, vmem_limit_bytes=60 * 2**20
        ),
        name="ranker",
    )(
        candidates.reshape(users * per_dev, width),
        behav_keys,
        behav_values,
        w_query,
        w_hidden,
        w_out.reshape(1, hid),
        jnp.transpose(clicks),
    )
    return jnp.transpose(logits), grad_hidden, grad_out.reshape(hid)


def solution(mesh):
    return jax.shard_map(
        functools.partial(on_device, mesh.shape["seq"], mesh.shape["grp"]),
        mesh=mesh,
        in_specs=(
            P("grp", "seq", None),
            P("grp", "seq", None),
            P("grp", "seq", None),
            P(),
            P(),
            P(),
            P("grp", "seq"),
        ),
        out_specs=(P("grp", "seq"), P(), P()),
        check_vma=False,
    )
```

```python
import functools
import math

import jax
import jax.numpy as jnp
from jax import lax
from jax.experimental import pallas as pl
from jax.experimental.pallas import tpu as pltpu
from jax.sharding import PartitionSpec as P

HEADS = 4
MESH = pl.DeviceIdType.MESH
NT = (((1,), (1,)), ((), ()))
F32 = jnp.float32
BF16 = jnp.bfloat16
GATHER, GATHER_TWIN, PARTIAL, TWIN_HEAD, REDUCE, OUT_X, LOGITS, OUT_GRP, GRP, OUT_ZY, ALL, ALL_TWIN, OUT_TWIN = (
    0, 2, 4, 5, 6, 7, 8, 9, 10, 11, 12, 13, 14
)
PHASES = 15
CHUNK = 512


def kernel(
    nc,
    ng,
    cand_hbm,
    keys_hbm,
    vals_hbm,
    wq_hbm,
    wh_hbm,
    wout_hbm,
    clicks_hbm,
    logits_ref,
    gh_ref,
    go_ref,
    x_buf,
    xf,
    qf,
    k_buf,
    v_buf,
    s_even,
    s_odd,
    q_heads,
    wq_buf,
    wh_buf,
    wout_ref,
    clicks_ref,
    clk,
    mine,
    theirs,
    p_send,
    p_recv,
    h_send,
    h_recv,
    g_send,
    g_recv,
    z_buf,
    ga_buf,
    l_send,
    l_recv,
    o1,
    o2,
    o3,
    o4,
    kv_sems,
    w_sems,
    twin_sems,
    twin_send_sem,
    send_sems,
    recv_sems,
):
    me = lax.axis_index("seq")
    grp = lax.axis_index("grp")
    core = lax.rem(me, 2)
    chip = me // 2
    users, length, width = k_buf.shape
    half_users = users // 2
    u_me = me // 4
    c_me = lax.rem(chip, 2)
    first_half = 1 - u_me // half_users
    head_size = width // HEADS
    scale = math.log2(math.e) / math.sqrt(head_size)
    hw = HEADS * width

    def user_at(t):
        return lax.rem(first_half + t // half_users, 2) * half_users + lax.rem(
            u_me + 1 + t, half_users
        )

    def on_chip(k):
        return lax.rem(chip + k, nc)

    def remote(src, dst, phase, seq, group=None):
        where = {"seq": seq} if group is None else {"seq": seq, "grp": group}
        return pltpu.make_async_remote_copy(
            src_ref=src,
            dst_ref=dst,
            send_sem=send_sems.at[phase],
            recv_sem=recv_sems.at[phase],
            device_id=where,
            device_id_type=MESH,
        )

    twin = chip * 2 + 1 - core

    def same_core(other_chip):
        return other_chip * 2 + core

    def local(src, dst, sem):
        return pltpu.make_async_copy(src, dst, sem)

    def wait_send(ref, phase):
        local(ref, ref, send_sems.at[phase]).wait()

    def wait_recv(ref, phase):
        local(ref, ref, recv_sems.at[phase]).wait()

    own_loads = [
        local(cand_hbm.at[pl.ds(16 * i, 16)], x_buf.at[i, core * nc + chip], w_sems.at[i])
        for i in range(2)
    ]
    for load in own_loads:
        load.start()
    wq_load = local(wq_hbm, wq_buf, w_sems.at[2])
    wq_load.start()
    clicks_load = local(clicks_hbm, clicks_ref, w_sems.at[4])
    clicks_load.start()

    @pl.loop(0, users)
    def _(t):
        u = user_at(t)
        local(keys_hbm.at[u], k_buf.at[u], kv_sems.at[0, t]).start()
        local(vals_hbm.at[u], v_buf.at[u], kv_sems.at[1, t]).start()

    wh_load = local(wh_hbm, wh_buf, w_sems.at[3])
    wh_load.start()
    wout_load = local(wout_hbm, wout_ref, w_sems.at[5])
    wout_load.start()

    barrier = pltpu.get_barrier_semaphore()
    pl.semaphore_signal(barrier, inc=1, device_id={"seq": twin}, device_id_type=MESH)

    @pl.loop(1, nc)
    def _(k):
        pl.semaphore_signal(
            barrier, inc=1, device_id={"seq": same_core(on_chip(k))}, device_id_type=MESH
        )

    for k in range(1, ng):
        pl.semaphore_signal(
            barrier,
            inc=1,
            device_id={"seq": me, "grp": lax.rem(grp + k, ng)},
            device_id_type=MESH,
        )

    clicks_load.wait()
    row_u = lax.broadcasted_iota(jnp.int32, (users, users), 0)
    col_u = lax.broadcasted_iota(jnp.int32, (users, users), 1)
    for c in range(2):
        wide = jnp.broadcast_to(clicks_ref[c : c + 1, :].astype(F32), (users, users))
        column = jnp.sum(jnp.where(row_u == col_u, wide, 0.0), axis=1, keepdims=True)
        clk[c] = jnp.broadcast_to(column, (users, width))

    pl.semaphore_wait(barrier, nc + ng - 1)

    for load in own_loads:
        load.wait()
    own = core * nc + chip
    for turn in range(2):

        @pl.loop(1, nc)
        def _(k):
            to = on_chip(k)
            part = lax.rem(to // (nc // 2) + 1 + turn, 2)
            remote(
                x_buf.at[part, own], x_buf.at[part, own], GATHER + part, same_core(to)
            ).start()

    def pass_on(part):
        wait_recv(x_buf.at[0, pl.ds(0, nc - 1)], GATHER + part)
        block = x_buf.at[part, pl.ds(core * nc, nc)]
        remote(block, block, GATHER_TWIN + part, twin).start()

    def make_queries(part):
        wait_recv(x_buf.at[0, pl.ds(0, nc)], GATHER_TWIN + part)
        x_all = x_buf[part].reshape(2 * nc * 16, width)
        queries = jnp.dot(x_all, wq_buf[...], preferred_element_type=F32)
        qf[part] = queries.astype(BF16).astype(F32)

    second_half = 1 - first_half
    wq_load.wait()
    pass_on(first_half)
    make_queries(first_half)

    head_of = lax.broadcasted_iota(jnp.int32, (2 * nc, width), 1) // head_size
    lane8 = lax.broadcasted_iota(jnp.int32, (8, width), 1)
    row8 = lax.broadcasted_iota(jnp.int32, (8, width), 0)
    group8 = lax.rem(lane8, head_size) // 8
    is_lse = lax.rem(lane8, 8) == 0
    is_click = lax.rem(lane8, 8) == 1
    at_me = (row8 == lax.rem(chip, 8)) & (group8 == chip // 8) & is_click

    def set_queries(u):
        part = u // half_users
        for c in range(2):
            rows = qf[part, pl.ds(lax.rem(u, half_users) * 2 + c, 2 * nc, stride=16), :]
            for h in range(HEADS):
                first = h * width + c * 2 * nc
                q_heads[first : first + 2 * nc, :] = jnp.where(head_of == h, rows, 0.0).astype(
                    BF16
                )

    def scores(u, j, s_ref, highest):
        rows = slice(j * CHUNK, j * CHUNK + CHUNK)
        s = lax.dot_general(k_buf[u, rows, :], q_heads[...], NT, preferred_element_type=F32)
        s_ref[rows, :] = s
        return jnp.maximum(highest, jnp.max(s.reshape(CHUNK // 8, 8, hw), axis=0))

    lowest = jnp.full((8, hw), -jnp.inf, F32)

    def attend(t, s_ref, s_next, highest, more=True):
        u = user_at(t)
        top = jnp.max(highest, axis=0, keepdims=True) * scale
        local(vals_hbm.at[u], v_buf.at[u], kv_sems.at[1, t]).wait()
        vals = jnp.transpose(v_buf[u])
        if more:
            u_next = user_at(t + 1)
            local(keys_hbm.at[u_next], k_buf.at[u_next], kv_sems.at[0, t + 1]).wait()
            set_queries(u_next)
        highest = lowest
        den = jnp.zeros((8, hw), F32)
        num = [jnp.zeros((2 * head_size, 2 * width), F32) for _ in range(HEADS // 2)]
        for j in range(length // CHUNK):
            if more:
                highest = scores(u_next, j, s_next, highest)
            rows = slice(j * CHUNK, j * CHUNK + CHUNK)
            p = jnp.exp2(s_ref[rows, :] * scale - top)
            den = den + jnp.sum(p.reshape(CHUNK // 8, 8, hw), axis=0)
            probs = p.astype(BF16)
            for h in range(HEADS // 2):
                num[h] = num[h] + jnp.dot(
                    vals[2 * head_size * h : 2 * head_size * (h + 1), rows],
                    probs[:, 2 * width * h : 2 * width * (h + 1)],
                    preferred_element_type=F32,
                )
        den = jnp.sum(den, axis=0, keepdims=True)
        inverse = 1.0 / den
        lse = top + jnp.log2(den)
        att_rows, lse_rows = [], []
        for h in range(HEADS):
            cols = slice(width * h, width * (h + 1))
            sub, at = head_size * (h % 2), width * (h % 2)
            block = num[h // 2][sub : sub + head_size, at : at + width]
            att_rows.append(block * inverse[:, cols])
            lse_rows.append(jnp.broadcast_to(lse[:, cols], (head_size, width)))
        att = jnp.transpose(jnp.concatenate(att_rows, axis=0))
        lse = jnp.transpose(jnp.concatenate(lse_rows, axis=0))
        for c in range(2):
            for half in range(2):
                first = 64 * c + 32 * half
                mine[t, half, c, 0:32] = att[first : first + 32]
                mine[t, half, c, 32:64] = lse[first : first + 32]
        pltpu.make_async_remote_copy(
            src_ref=mine.at[t, 1 - core],
            dst_ref=theirs.at[t],
            send_sem=twin_send_sem,
            recv_sem=twin_sems.at[t],
            device_id={"seq": twin},
            device_id_type=MESH,
        ).start()
        return highest

    def merge(t):
        u = user_at(t)
        local(theirs.at[t], theirs.at[t], twin_sems.at[t]).wait()
        for c in range(2):
            a, b = mine[t, core, c], theirs[t, c]
            top = jnp.maximum(a[32:64], b[32:64])
            wa, wb = jnp.exp2(a[32:64] - top), jnp.exp2(b[32:64] - top)
            total = wa + wb
            lse = top + jnp.log2(total)
            slot = t * 2 + c
            p_send[slot, 0:32] = (a[0:32] * wa + b[0:32] * wb) / total
            tile = jnp.zeros((8, width), F32)
            for g in range(4):
                tile = jnp.where(is_lse & (group8 == g), lse[8 * g : 8 * g + 8], tile)
            click = jnp.broadcast_to(clk[c, pl.ds(u, 1), :], (8, width))
            p_send[slot, 32:40] = jnp.where(at_me, click, tile)
            to = 4 * u + 2 * c + core

            @pl.when(to != me)
            def _():
                remote(p_send.at[slot], p_recv.at[chip], PARTIAL, to).start()

            @pl.when(to == me)
            def _():
                local(p_send.at[slot], p_recv.at[chip], recv_sems.at[PARTIAL]).start()

    u_first = user_at(0)
    local(keys_hbm.at[u_first], k_buf.at[u_first], kv_sems.at[0, 0]).wait()
    set_queries(u_first)
    highest = lowest
    for j in range(length // CHUNK):
        highest = scores(u_first, j, s_even, highest)

    def two_users(i, highest):
        t = 2 * i

        @pl.when(i == 1)
        def _():
            pass_on(second_half)

        highest = attend(t, s_even, s_odd, highest)

        @pl.when(i > 0)
        def _():
            merge(t - 1)

        @pl.when(i == half_users // 2 - 1)
        def _():
            make_queries(second_half)
            xf[...] = x_buf[second_half].reshape(2 * nc * 16, width).astype(F32)

        highest = attend(t + 1, s_odd, s_even, highest)
        merge(t)
        return highest

    highest = lax.fori_loop(0, users // 2 - 1, two_users, highest)
    highest = attend(users - 2, s_even, s_odd, highest)
    merge(users - 3)
    attend(users - 1, s_odd, None, highest, more=False)
    merge(users - 2)
    merge(users - 1)

    wait_recv(p_recv, PARTIAL)
    ej = lax.broadcasted_iota(jnp.int32, (width, 4 * width), 0)
    ef = lax.broadcasted_iota(jnp.int32, (width, 4 * width), 1)
    same = (ej // head_size == lax.rem(ef, width) // head_size) & (
        lax.rem(ej, head_size) // 8 == ef // width
    )
    spread = jnp.where(same & (lax.rem(ej, 8) == 0), 1.0, 0.0).astype(BF16)
    spread_click = jnp.where(same & (lax.rem(ej, 8) == 1), 1.0, 0.0).astype(BF16)
    tiles = p_recv[:, 32:40, :]
    rest = tiles.reshape(nc * 8, width)
    lse_all = jnp.zeros((nc * 8, 4 * width), F32)
    for _ in range(3):
        piece = rest.astype(BF16)
        rest = rest - piece.astype(F32)
        lse_all = lse_all + jnp.dot(piece, spread, preferred_element_type=F32)
    lse_all = lse_all.reshape(nc, 8, 4 * width)
    w = jnp.exp2(lse_all - jnp.max(lse_all, axis=0)[None])
    den = jnp.sum(w, axis=0)
    attended = []
    for g in range(4):
        cols = slice(g * width, g * width + width)
        num = jnp.sum(p_recv[:, 8 * g : 8 * g + 8, :] * w[:, :, cols], axis=0)
        attended.append(num / den[:, cols])
    attended = jnp.concatenate(attended, axis=0).astype(BF16).astype(F32)
    click_tile = jnp.where(is_click, jnp.sum(tiles, axis=0), 0.0)
    click = jnp.dot(click_tile.astype(BF16), spread_click, preferred_element_type=F32)
    click = jnp.concatenate([click[:, g * width : g * width + width] for g in range(4)], axis=0)
    click = click[:, 0:1]

    def candidates_of(which):
        first = which * nc * 16 + lax.rem(u_me, half_users) * 2 + c_me
        return xf[pl.ds(first, nc, stride=16), :]

    features = jnp.concatenate([candidates_of(core), attended], axis=1)
    wh_load.wait()
    wout_load.wait()
    pre = jnp.dot(features.astype(BF16), wh_buf[...], preferred_element_type=F32)
    hidden = jnp.maximum(pre, 0.0).astype(BF16).astype(F32)
    logits = jnp.sum(hidden * wout_ref[...], axis=-1, keepdims=True)
    dlogit = 1.0 / (1.0 + jnp.exp(-logits)) - click
    h_send[0:32] = attended
    h_send[32:64] = jnp.broadcast_to(dlogit, (nc, width))
    remote(h_send, h_recv, TWIN_HEAD, twin).start()

    half_hid = wh_buf.shape[1] // 2
    my_cols = pl.ds(pl.multiple_of(core * half_hid, half_hid), half_hid)
    wout = wout_ref[:, my_cols]

    def half_of(a):
        return jnp.where(core == 0, a[:, :half_hid], a[:, half_hid:])

    def dpre_of(pre, dlogit):
        return jnp.where(pre > 0.0, dlogit * wout, 0.0).astype(BF16)

    dpre = dpre_of(half_of(pre), dlogit)
    out_part = jnp.sum(half_of(hidden) * dlogit, axis=0, keepdims=True)
    wait_recv(h_recv, TWIN_HEAD)
    other = jnp.concatenate([candidates_of(1 - core), h_recv[0:32]], axis=1)
    dlogit = h_recv[32:64, 0:1]
    pre = jnp.dot(other.astype(BF16), wh_buf[:, my_cols], preferred_element_type=F32)
    hidden = jnp.maximum(pre, 0.0).astype(BF16).astype(F32)
    out_part = out_part + jnp.sum(hidden * dlogit, axis=0, keepdims=True)
    features = jnp.concatenate([features, other], axis=0)
    dpre = jnp.concatenate([dpre, dpre_of(pre, dlogit)], axis=0)
    grad = jnp.dot(jnp.transpose(features).astype(BF16), dpre, preferred_element_type=F32)
    bw = half_hid // 2
    for b in range(nc):
        i, j = b // 2, b % 2
        g_send[b] = grad[16 * i : 16 * i + 16, bw * j : bw * j + bw].astype(BF16)

    @pl.loop(1, nc)
    def _(k):
        to = on_chip(k)
        remote(g_send.at[to], g_recv.at[chip], REDUCE, same_core(to)).start()

    g_recv[chip] = g_send[chip]

    at_x, at_zy = lax.rem(chip, 4), chip // 4
    pieces = [out_part[:, width * i : width * i + width] for i in range(4)]
    o1[at_x] = jnp.concatenate(pieces + [jnp.zeros((4, width), F32)], axis=0)
    for k in range(1, 4):
        to = at_zy * 4 + lax.rem(at_x + k, 4)
        remote(o1.at[at_x], o1.at[at_x], OUT_X, same_core(to)).start()

    wide = jnp.broadcast_to(logits, (nc, width))
    for i in range(nc):
        l_send[i] = wide[i : i + 1, :]
    l_slot = c_me * users + u_me

    @pl.loop(1, nc)
    def _(k):
        to = on_chip(k)
        remote(l_send.at[to], l_recv.at[l_slot], LOGITS, same_core(to)).start()

    l_recv[l_slot] = l_send[chip]

    wait_recv(o1.at[pl.ds(0, 3)], OUT_X)
    o2[grp] = o1[0] + o1[1] + o1[2] + o1[3]
    for k in range(1, ng):
        remote(o2.at[grp], o2.at[grp], OUT_GRP, me, lax.rem(grp + k, ng)).start()
    wait_recv(g_recv.at[pl.ds(0, nc - 1)], REDUCE)
    z_buf[grp] = jnp.sum(g_recv[...].astype(F32), axis=0)
    for k in range(1, ng):
        remote(z_buf.at[grp], z_buf.at[grp], GRP, me, lax.rem(grp + k, ng)).start()
    wait_recv(o2.at[pl.ds(0, ng - 1)], OUT_GRP)
    o3[at_zy] = jnp.sum(o2[...], axis=0)
    for k in range(1, 8):
        to = lax.rem(at_zy + k, 8) * 4 + at_x
        remote(o3.at[at_zy], o3.at[at_zy], OUT_ZY, same_core(to)).start()
    wait_recv(z_buf.at[pl.ds(0, ng - 1)], GRP)
    ga_buf[core, chip] = jnp.sum(z_buf[...], axis=0).astype(BF16)

    @pl.loop(1, nc)
    def _(k):
        block = ga_buf.at[core, chip]
        remote(block, block, ALL, same_core(on_chip(k))).start()

    wait_recv(l_recv.at[pl.ds(0, nc - 1)], LOGITS)
    logit_rows = l_recv[...].reshape(2 * users, width)
    row_o = lax.broadcasted_iota(jnp.int32, (users, width), 0)
    col_o = lax.broadcasted_iota(jnp.int32, (users, width), 1)
    for c in range(2):
        rows = jnp.where(row_o == col_o, logit_rows[users * c : users * (c + 1)], 0.0)
        logits_ref[c : c + 1, :] = jnp.sum(rows, axis=0, keepdims=True)[:, :users]
    wait_recv(o3.at[pl.ds(0, 7)], OUT_ZY)
    o4[core] = jnp.sum(o3[...], axis=0)
    remote(o4.at[core], o4.at[core], OUT_TWIN, twin).start()

    for part in range(2):
        wait_send(x_buf.at[0, pl.ds(0, nc - 1)], GATHER + part)
        wait_send(x_buf.at[0, pl.ds(0, nc)], GATHER_TWIN + part)
    local(theirs, theirs, twin_send_sem).wait()
    wait_send(p_send.at[pl.ds(0, nc - 1)], PARTIAL)
    wait_send(h_send, TWIN_HEAD)
    wait_send(l_send.at[pl.ds(0, nc - 1)], LOGITS)
    wait_send(g_send.at[pl.ds(0, nc - 1)], REDUCE)
    wait_send(o1.at[pl.ds(0, 3)], OUT_X)
    wait_send(o2.at[pl.ds(0, ng - 1)], OUT_GRP)
    wait_send(z_buf.at[pl.ds(0, ng - 1)], GRP)
    wait_send(o3.at[pl.ds(0, 7)], OUT_ZY)

    wait_recv(ga_buf.at[0, pl.ds(0, nc - 1)], ALL)
    remote(ga_buf.at[core], ga_buf.at[core], ALL_TWIN, twin).start()

    def write(side):
        for j in range(2):
            cols = pl.ds(pl.multiple_of(side * half_hid + j * bw, bw), bw)
            for i in range(nc // 2):
                gh_ref[16 * i : 16 * i + 16, cols] = ga_buf[side, 2 * i + j].astype(F32)

    write(core)
    wait_recv(o4.at[0], OUT_TWIN)
    go_ref[...] = jnp.concatenate([o4[0, 0:4], o4[1, 0:4]], axis=0)
    wait_recv(ga_buf.at[0], ALL_TWIN)
    write(1 - core)
    wait_send(ga_buf.at[0, pl.ds(0, nc - 1)], ALL)
    wait_send(ga_buf.at[0], ALL_TWIN)
    wait_send(o4.at[0], OUT_TWIN)


def on_device(ns, ng, candidates, behav_keys, behav_values, w_query, w_hidden, w_out, clicks):
    users, per_dev, width = candidates.shape
    length = behav_keys.shape[1]
    feats, hid = w_hidden.shape
    nc = ns // 2
    hbm_spec = pl.BlockSpec(memory_space=pltpu.HBM)
    vmem_spec = pl.BlockSpec(memory_space=pltpu.VMEM)
    logits, grad_hidden, grad_out = pl.pallas_call(
        functools.partial(kernel, nc, ng),
        out_shape=(
            jax.ShapeDtypeStruct((per_dev, users), F32),
            jax.ShapeDtypeStruct((feats, hid), F32),
            jax.ShapeDtypeStruct((8, width), F32),
        ),
        in_specs=[hbm_spec] * 7,
        out_specs=(vmem_spec, vmem_spec, vmem_spec),
        scratch_shapes=[
            pltpu.VMEM((2, ns, 16, width), BF16),
            pltpu.VMEM((ns * 16, width), F32),
            pltpu.VMEM((2, ns * 16, width), F32),
            pltpu.VMEM((users, length, width), BF16),
            pltpu.VMEM((users, length, width), BF16),
            pltpu.VMEM((length, HEADS * width), F32),
            pltpu.VMEM((length, HEADS * width), F32),
            pltpu.VMEM((HEADS * width, width), BF16),
            pltpu.VMEM((width, width), BF16),
            pltpu.VMEM((feats, hid), BF16),
            pltpu.VMEM((1, hid), F32),
            pltpu.VMEM((per_dev, users), jnp.int32),
            pltpu.VMEM((per_dev, users, width), F32),
            pltpu.VMEM((users, 2, 2, 64, width), F32),
            pltpu.VMEM((users, 2, 64, width), F32),
            pltpu.VMEM((nc, 40, width), F32),
            pltpu.VMEM((nc, 40, width), F32),
            pltpu.VMEM((64, width), F32),
            pltpu.VMEM((64, width), F32),
            pltpu.VMEM((nc, 16, hid // 4), BF16),
            pltpu.VMEM((nc, 16, hid // 4), BF16),
            pltpu.VMEM((ng, 16, hid // 4), F32),
            pltpu.VMEM((2, nc, 16, hid // 4), BF16),
            pltpu.VMEM((nc, 1, width), F32),
            pltpu.VMEM((nc, 1, width), F32),
            pltpu.VMEM((4, 8, width), F32),
            pltpu.VMEM((ng, 8, width), F32),
            pltpu.VMEM((8, 8, width), F32),
            pltpu.VMEM((2, 8, width), F32),
            pltpu.SemaphoreType.DMA((2, users)),
            pltpu.SemaphoreType.DMA((6,)),
            pltpu.SemaphoreType.DMA((users,)),
            pltpu.SemaphoreType.DMA,
            pltpu.SemaphoreType.DMA((PHASES,)),
            pltpu.SemaphoreType.DMA((PHASES,)),
        ],
        compiler_params=pltpu.CompilerParams(
            collective_id=0, has_side_effects=True, vmem_limit_bytes=40 * 2**20
        ),
        name="ranker",
    )(
        *(
            pltpu.with_memory_space_constraint(operand, pltpu.HBM)
            for operand in (
                candidates.reshape(users * per_dev, width),
                behav_keys,
                behav_values,
                w_query,
                w_hidden,
                w_out.reshape(1, hid),
                jnp.transpose(clicks),
            )
        )
    )
    return jnp.transpose(logits), grad_hidden, grad_out.reshape(hid)


def solution(mesh):
    return jax.shard_map(
        functools.partial(on_device, mesh.shape["seq"], mesh.shape["grp"]),
        mesh=mesh,
        in_specs=(
            P("grp", "seq", None),
            P("grp", "seq", None),
            P("grp", "seq", None),
            P(),
            P(),
            P(),
            P("grp", "seq"),
        ),
        out_specs=(P("grp", "seq"), P(), P()),
        check_vma=False,
    )
```

```python
import functools
import math

import jax
import jax.numpy as jnp
from jax import lax
from jax.experimental import pallas as pl
from jax.experimental.pallas import tpu as pltpu
from jax.sharding import PartitionSpec as P

HEADS = 4
MESH = pl.DeviceIdType.MESH
NT = (((1,), (1,)), ((), ()))
F32 = jnp.float32
BF16 = jnp.bfloat16
GATHER, GATHER_TWIN, PARTIAL, TWIN_HEAD, REDUCE, OUT_X, LOGITS, OUT_GRP, GRP, OUT_ZY, ALL, ALL_TWIN, OUT_TWIN = (
    0, 2, 4, 5, 6, 7, 8, 9, 10, 11, 12, 13, 14
)
PHASES = 15
CHUNK = 1024
DIRECT = 3


def kernel(
    nc,
    ng,
    cand_hbm,
    keys_hbm,
    vals_hbm,
    wq_hbm,
    wh_hbm,
    wout_hbm,
    clicks_hbm,
    logits_ref,
    gh_ref,
    go_ref,
    x_buf,
    xf,
    qf,
    k_buf,
    v_buf,
    s_even,
    s_odd,
    q_heads,
    wq_buf,
    wh_buf,
    wout_ref,
    clicks_ref,
    clk,
    raw,
    mine,
    theirs,
    p_send,
    p_recv,
    h_send,
    h_recv,
    g_send,
    g_recv,
    z_buf,
    ga_buf,
    l_send,
    l_recv,
    o1,
    o2,
    o3,
    o4,
    kv_sems,
    w_sems,
    twin_sems,
    twin_send_sem,
    send_sems,
    recv_sems,
):
    me = lax.axis_index("seq")
    grp = lax.axis_index("grp")
    core = lax.rem(me, 2)
    chip = me // 2
    users, length, width = k_buf.shape
    half_users = users // 2
    u_me = me // 4
    c_me = lax.rem(chip, 2)
    first_half = 1 - u_me // half_users
    head_size = width // HEADS
    scale = math.log2(math.e) / math.sqrt(head_size)
    hw = HEADS * width

    def user_at(t):
        return lax.rem(first_half + t // half_users, 2) * half_users + lax.rem(
            u_me + 1 + t, half_users
        )

    def on_chip(k):
        return lax.rem(chip + k, nc)

    def remote(src, dst, phase, seq, group=None):
        where = {"seq": seq} if group is None else {"seq": seq, "grp": group}
        return pltpu.make_async_remote_copy(
            src_ref=src,
            dst_ref=dst,
            send_sem=send_sems.at[phase],
            recv_sem=recv_sems.at[phase],
            device_id=where,
            device_id_type=MESH,
        )

    twin = chip * 2 + 1 - core

    def same_core(other_chip):
        return other_chip * 2 + core

    def local(src, dst, sem):
        return pltpu.make_async_copy(src, dst, sem)

    def wait_send(ref, phase):
        local(ref, ref, send_sems.at[phase]).wait()

    def wait_recv(ref, phase):
        local(ref, ref, recv_sems.at[phase]).wait()

    own_loads = [
        local(cand_hbm.at[pl.ds(16 * i, 16)], x_buf.at[i, core * nc + chip], w_sems.at[i])
        for i in range(2)
    ]
    for load in own_loads:
        load.start()
    wq_load = local(wq_hbm, wq_buf, w_sems.at[2])
    wq_load.start()
    clicks_load = local(clicks_hbm, clicks_ref, w_sems.at[4])
    clicks_load.start()

    @pl.loop(0, users)
    def _(t):
        u = user_at(t)
        local(keys_hbm.at[u], k_buf.at[u], kv_sems.at[0, t]).start()
        local(vals_hbm.at[u], v_buf.at[u], kv_sems.at[1, t]).start()

    wh_load = local(wh_hbm, wh_buf, w_sems.at[3])
    wh_load.start()
    wout_load = local(wout_hbm, wout_ref, w_sems.at[5])
    wout_load.start()

    barrier = pltpu.get_barrier_semaphore()
    pl.semaphore_signal(barrier, inc=1, device_id={"seq": twin}, device_id_type=MESH)

    @pl.loop(1, nc)
    def _(k):
        pl.semaphore_signal(
            barrier, inc=1, device_id={"seq": same_core(on_chip(k))}, device_id_type=MESH
        )

    for k in range(1, ng):
        pl.semaphore_signal(
            barrier,
            inc=1,
            device_id={"seq": me, "grp": lax.rem(grp + k, ng)},
            device_id_type=MESH,
        )

    half_base = (u_me // half_users) * half_users
    for d in range(1, DIRECT):
        u = half_base + lax.rem(u_me + d, half_users)
        for c in range(2):
            pl.semaphore_signal(
                barrier,
                inc=1,
                device_id={"seq": 4 * u + 2 * c + 1 - core},
                device_id_type=MESH,
            )
    pl.semaphore_signal(
        barrier,
        inc=1,
        device_id={"seq": 4 * u_me + 2 * (1 - c_me) + 1 - core},
        device_id_type=MESH,
    )

    clicks_load.wait()
    row_u = lax.broadcasted_iota(jnp.int32, (users, users), 0)
    col_u = lax.broadcasted_iota(jnp.int32, (users, users), 1)
    for c in range(2):
        wide = jnp.broadcast_to(clicks_ref[c : c + 1, :].astype(F32), (users, users))
        column = jnp.sum(jnp.where(row_u == col_u, wide, 0.0), axis=1, keepdims=True)
        clk[c] = jnp.broadcast_to(column, (users, width))

    pl.semaphore_wait(barrier, nc + ng - 1 + 2 * (DIRECT - 1) + 1)

    for load in own_loads:
        load.wait()
    own = core * nc + chip
    for turn in range(2):

        @pl.loop(1, nc)
        def _(k):
            to = on_chip(k)
            part = lax.rem(to // (nc // 2) + 1 + turn, 2)
            remote(
                x_buf.at[part, own], x_buf.at[part, own], GATHER + part, same_core(to)
            ).start()

    def pass_on(part):
        wait_recv(x_buf.at[0, pl.ds(0, nc - 1)], GATHER + part)
        block = x_buf.at[part, pl.ds(core * nc, nc)]
        remote(block, block, GATHER_TWIN + part, twin).start()

    def make_queries(part):
        wait_recv(x_buf.at[0, pl.ds(0, nc)], GATHER_TWIN + part)
        x_all = x_buf[part].reshape(2 * nc * 16, width)
        queries = jnp.dot(x_all, wq_buf[...], preferred_element_type=F32)
        qf[part] = queries.astype(BF16).astype(F32)

    second_half = 1 - first_half
    wq_load.wait()
    pass_on(first_half)
    make_queries(first_half)

    head_of = lax.broadcasted_iota(jnp.int32, (2 * nc, width), 1) // head_size
    lane8 = lax.broadcasted_iota(jnp.int32, (8, width), 1)
    row8 = lax.broadcasted_iota(jnp.int32, (8, width), 0)
    group8 = lax.rem(lane8, head_size) // 8
    is_lse = lax.rem(lane8, 8) == 0
    is_click = lax.rem(lane8, 8) == 1
    at_me = (row8 == lax.rem(chip, 8)) & (group8 == chip // 8) & is_click

    def set_queries(u):
        part = u // half_users
        for c in range(2):
            rows = qf[part, pl.ds(lax.rem(u, half_users) * 2 + c, 2 * nc, stride=16), :]
            for h in range(HEADS):
                first = h * width + c * 2 * nc
                q_heads[first : first + 2 * nc, :] = jnp.where(head_of == h, rows, 0.0).astype(
                    BF16
                )

    def scores(u, j, s_ref, highest):
        rows = slice(j * CHUNK, j * CHUNK + CHUNK)
        s = lax.dot_general(k_buf[u, rows, :], q_heads[...], NT, preferred_element_type=F32)
        s_ref[rows, :] = s
        return jnp.maximum(highest, jnp.max(s.reshape(CHUNK // 8, 8, hw), axis=0))

    lowest = jnp.full((8, hw), -jnp.inf, F32)

    def finished():
        return jnp.transpose(raw[0]), jnp.transpose(raw[1])

    def to_twin(t):
        pltpu.make_async_remote_copy(
            src_ref=mine.at[t, 1 - core],
            dst_ref=theirs.at[t],
            send_sem=twin_send_sem,
            recv_sem=twin_sems.at[t],
            device_id={"seq": twin},
            device_id_type=MESH,
        ).start()

    def to_owner(slot, to, into, att, lse, click_row):
        p_send[slot, 0:32] = att
        tile = jnp.zeros((8, width), F32)
        for g in range(4):
            tile = jnp.where(is_lse & (group8 == g), lse[8 * g : 8 * g + 8], tile)
        click = jnp.broadcast_to(click_row, (8, width))
        p_send[slot, 32:40] = jnp.where(at_me, click, tile)

        @pl.when(to != me)
        def _():
            remote(p_send.at[slot], p_recv.at[into], PARTIAL, to).start()

        @pl.when(to == me)
        def _():
            local(p_send.at[slot], p_recv.at[into], recv_sems.at[PARTIAL]).start()

    def attend(t, s_ref, s_next, highest, more=True, before=None):
        u = user_at(t)
        if before is not None:
            att, lse = finished()
            for c in range(2):
                for half in range(2):
                    first = 64 * c + 32 * half
                    mine[before, half, c, 0:32] = att[first : first + 32]
                    mine[before, half, c, 32:64] = lse[first : first + 32]
        top = jnp.max(highest, axis=0, keepdims=True) * scale
        local(vals_hbm.at[u], v_buf.at[u], kv_sems.at[1, t]).wait()
        vals = jnp.transpose(v_buf[u])
        if more:
            u_next = user_at(t + 1)
            local(keys_hbm.at[u_next], k_buf.at[u_next], kv_sems.at[0, t + 1]).wait()
            set_queries(u_next)
        highest = lowest
        den = jnp.zeros((8, hw), F32)
        num = [jnp.zeros((2 * head_size, 2 * width), F32) for _ in range(HEADS // 2)]
        for j in range(length // CHUNK):
            if more:
                highest = scores(u_next, j, s_next, highest)
            rows = slice(j * CHUNK, j * CHUNK + CHUNK)
            p = jnp.exp2(s_ref[rows, :] * scale - top)
            den = den + jnp.sum(p.reshape(CHUNK // 8, 8, hw), axis=0)
            probs = p.astype(BF16)
            for h in range(HEADS // 2):
                num[h] = num[h] + jnp.dot(
                    vals[2 * head_size * h : 2 * head_size * (h + 1), rows],
                    probs[:, 2 * width * h : 2 * width * (h + 1)],
                    preferred_element_type=F32,
                )
        den = jnp.sum(den, axis=0, keepdims=True)
        inverse = 1.0 / den
        lse = top + jnp.log2(den)
        for h in range(HEADS):
            cols = slice(width * h, width * (h + 1))
            rows = slice(head_size * h, head_size * (h + 1))
            sub, at = head_size * (h % 2), width * (h % 2)
            block = num[h // 2][sub : sub + head_size, at : at + width]
            raw[0, rows, :] = block * inverse[:, cols]
            raw[1, rows, :] = jnp.broadcast_to(lse[:, cols], (head_size, width))
        return highest

    def merge(t):
        u = user_at(t)
        local(theirs.at[t], theirs.at[t], twin_sems.at[t]).wait()
        for c in range(2):
            a, b = mine[t, core, c], theirs[t, c]
            top = jnp.maximum(a[32:64], b[32:64])
            wa, wb = jnp.exp2(a[32:64] - top), jnp.exp2(b[32:64] - top)
            total = wa + wb
            lse = top + jnp.log2(total)
            att = (a[0:32] * wa + b[0:32] * wb) / total
            to_owner(t * 2 + c, 4 * u + 2 * c + core, chip, att, lse, clk[c, pl.ds(u, 1), :])

    def unmerged(t):
        u = user_at(t)
        att, lse = finished()
        base = 2 * (users - DIRECT) + 4 * (t - (users - DIRECT))
        for c in range(2):
            for half in range(2):
                rows = slice(64 * c + 32 * half, 64 * c + 32 * half + 32)
                same = core == half
                into = jnp.where(same, chip, nc + 2 * (users - 1 - t) + c_me)
                click = clk[c, pl.ds(u, 1), :] * jnp.where(same, 1.0, 0.0)
                to = 4 * u + 2 * c + half
                to_owner(base + 2 * c + half, to, into, att[rows], lse[rows], click)

    u_first = user_at(0)
    local(keys_hbm.at[u_first], k_buf.at[u_first], kv_sems.at[0, 0]).wait()
    set_queries(u_first)
    highest = lowest
    for j in range(length // CHUNK):
        highest = scores(u_first, j, s_even, highest)

    def two_users(i, highest):
        t = 2 * i

        @pl.when(i == 1)
        def _():
            pass_on(second_half)

        highest = attend(t, s_even, s_odd, highest, before=jnp.maximum(t - 1, 0))

        @pl.when(i > 0)
        def _():
            to_twin(t - 1)

        @pl.when(i > 1)
        def _():
            merge(t - 3)

        @pl.when(i == half_users // 2 - 1)
        def _():
            make_queries(second_half)
            xf[...] = x_buf[second_half].reshape(2 * nc * 16, width).astype(F32)

        highest = attend(t + 1, s_odd, s_even, highest, before=t)
        to_twin(t)

        @pl.when(i > 0)
        def _():
            merge(t - 2)

        return highest

    raw[...] = jnp.zeros_like(raw)
    highest = lax.fori_loop(0, users // 2 - 1, two_users, highest)
    unmerged(users - 3)
    highest = attend(users - 2, s_even, s_odd, highest)
    merge(users - 5)
    unmerged(users - 2)
    attend(users - 1, s_odd, None, highest, more=False)
    merge(users - 4)
    unmerged(users - 1)

    wait_recv(p_recv, PARTIAL)
    ej = lax.broadcasted_iota(jnp.int32, (width, 4 * width), 0)
    ef = lax.broadcasted_iota(jnp.int32, (width, 4 * width), 1)
    same = (ej // head_size == lax.rem(ef, width) // head_size) & (
        lax.rem(ej, head_size) // 8 == ef // width
    )
    spread = jnp.where(same & (lax.rem(ej, 8) == 0), 1.0, 0.0).astype(BF16)
    spread_click = jnp.where(same & (lax.rem(ej, 8) == 1), 1.0, 0.0).astype(BF16)
    tiles = p_recv[:, 32:40, :]
    rest = tiles.reshape(p_recv.shape[0] * 8, width)
    senders = p_recv.shape[0]
    lse_all = jnp.zeros((senders * 8, 4 * width), F32)
    for _ in range(3):
        piece = rest.astype(BF16)
        rest = rest - piece.astype(F32)
        lse_all = lse_all + jnp.dot(piece, spread, preferred_element_type=F32)
    lse_all = lse_all.reshape(senders, 8, 4 * width)
    w = jnp.exp2(lse_all - jnp.max(lse_all, axis=0)[None])
    den = jnp.sum(w, axis=0)
    attended = []
    for g in range(4):
        cols = slice(g * width, g * width + width)
        num = jnp.sum(p_recv[:, 8 * g : 8 * g + 8, :] * w[:, :, cols], axis=0)
        attended.append(num / den[:, cols])
    attended = jnp.concatenate(attended, axis=0).astype(BF16).astype(F32)
    click_tile = jnp.where(is_click, jnp.sum(tiles, axis=0), 0.0)
    click = jnp.dot(click_tile.astype(BF16), spread_click, preferred_element_type=F32)
    click = jnp.concatenate([click[:, g * width : g * width + width] for g in range(4)], axis=0)
    click = click[:, 0:1]

    def candidates_of(which):
        first = which * nc * 16 + lax.rem(u_me, half_users) * 2 + c_me
        return xf[pl.ds(first, nc, stride=16), :]

    features = jnp.concatenate([candidates_of(core), attended], axis=1)
    wh_load.wait()
    wout_load.wait()
    pre = jnp.dot(features.astype(BF16), wh_buf[...], preferred_element_type=F32)
    hidden = jnp.maximum(pre, 0.0).astype(BF16).astype(F32)
    logits = jnp.sum(hidden * wout_ref[...], axis=-1, keepdims=True)
    dlogit = 1.0 / (1.0 + jnp.exp(-logits)) - click
    h_send[0:32] = attended
    h_send[32:64] = jnp.broadcast_to(dlogit, (nc, width))
    remote(h_send, h_recv, TWIN_HEAD, twin).start()

    half_hid = wh_buf.shape[1] // 2
    my_cols = pl.ds(pl.multiple_of(core * half_hid, half_hid), half_hid)
    wout = wout_ref[:, my_cols]

    def half_of(a):
        return jnp.where(core == 0, a[:, :half_hid], a[:, half_hid:])

    def dpre_of(pre, dlogit):
        return jnp.where(pre > 0.0, dlogit * wout, 0.0).astype(BF16)

    dpre = dpre_of(half_of(pre), dlogit)
    out_part = jnp.sum(half_of(hidden) * dlogit, axis=0, keepdims=True)
    wait_recv(h_recv, TWIN_HEAD)
    other = jnp.concatenate([candidates_of(1 - core), h_recv[0:32]], axis=1)
    dlogit = h_recv[32:64, 0:1]
    pre = jnp.dot(other.astype(BF16), wh_buf[:, my_cols], preferred_element_type=F32)
    hidden = jnp.maximum(pre, 0.0).astype(BF16).astype(F32)
    out_part = out_part + jnp.sum(hidden * dlogit, axis=0, keepdims=True)
    features = jnp.concatenate([features, other], axis=0)
    dpre = jnp.concatenate([dpre, dpre_of(pre, dlogit)], axis=0)
    grad = jnp.dot(jnp.transpose(features).astype(BF16), dpre, preferred_element_type=F32)
    bw = half_hid // 2
    for b in range(nc):
        i, j = b // 2, b % 2
        g_send[b] = grad[16 * i : 16 * i + 16, bw * j : bw * j + bw].astype(BF16)

    @pl.loop(1, nc)
    def _(k):
        to = on_chip(k)
        remote(g_send.at[to], g_recv.at[chip], REDUCE, same_core(to)).start()

    g_recv[chip] = g_send[chip]

    at_x, at_zy = lax.rem(chip, 4), chip // 4
    pieces = [out_part[:, width * i : width * i + width] for i in range(4)]
    o1[at_x] = jnp.concatenate(pieces + [jnp.zeros((4, width), F32)], axis=0)
    for k in range(1, 4):
        to = at_zy * 4 + lax.rem(at_x + k, 4)
        remote(o1.at[at_x], o1.at[at_x], OUT_X, same_core(to)).start()

    wide = jnp.broadcast_to(logits, (nc, width))
    for i in range(nc):
        l_send[i] = wide[i : i + 1, :]
    l_slot = c_me * users + u_me

    @pl.loop(1, nc)
    def _(k):
        to = on_chip(k)
        remote(l_send.at[to], l_recv.at[l_slot], LOGITS, same_core(to)).start()

    l_recv[l_slot] = l_send[chip]

    wait_recv(o1.at[pl.ds(0, 3)], OUT_X)
    o2[grp] = o1[0] + o1[1] + o1[2] + o1[3]
    for k in range(1, ng):
        remote(o2.at[grp], o2.at[grp], OUT_GRP, me, lax.rem(grp + k, ng)).start()
    wait_recv(g_recv.at[pl.ds(0, nc - 1)], REDUCE)
    z_buf[grp] = jnp.sum(g_recv[...].astype(F32), axis=0)
    for k in range(1, ng):
        remote(z_buf.at[grp], z_buf.at[grp], GRP, me, lax.rem(grp + k, ng)).start()
    wait_recv(o2.at[pl.ds(0, ng - 1)], OUT_GRP)
    o3[at_zy] = jnp.sum(o2[...], axis=0)
    for k in range(1, 8):
        to = lax.rem(at_zy + k, 8) * 4 + at_x
        remote(o3.at[at_zy], o3.at[at_zy], OUT_ZY, same_core(to)).start()
    wait_recv(z_buf.at[pl.ds(0, ng - 1)], GRP)
    ga_buf[core, chip] = jnp.sum(z_buf[...], axis=0).astype(BF16)

    @pl.loop(1, nc)
    def _(k):
        block = ga_buf.at[core, chip]
        remote(block, block, ALL, same_core(on_chip(k))).start()

    wait_recv(l_recv.at[pl.ds(0, nc - 1)], LOGITS)
    logit_rows = l_recv[...].reshape(2 * users, width)
    row_o = lax.broadcasted_iota(jnp.int32, (users, width), 0)
    col_o = lax.broadcasted_iota(jnp.int32, (users, width), 1)
    for c in range(2):
        rows = jnp.where(row_o == col_o, logit_rows[users * c : users * (c + 1)], 0.0)
        logits_ref[c : c + 1, :] = jnp.sum(rows, axis=0, keepdims=True)[:, :users]
    wait_recv(o3.at[pl.ds(0, 7)], OUT_ZY)
    o4[core] = jnp.sum(o3[...], axis=0)
    remote(o4.at[core], o4.at[core], OUT_TWIN, twin).start()

    for part in range(2):
        wait_send(x_buf.at[0, pl.ds(0, nc - 1)], GATHER + part)
        wait_send(x_buf.at[0, pl.ds(0, nc)], GATHER_TWIN + part)
    local(theirs, theirs, twin_send_sem).wait()
    wait_send(p_send.at[pl.ds(0, p_send.shape[0] - 1)], PARTIAL)
    wait_send(h_send, TWIN_HEAD)
    wait_send(l_send.at[pl.ds(0, nc - 1)], LOGITS)
    wait_send(g_send.at[pl.ds(0, nc - 1)], REDUCE)
    wait_send(o1.at[pl.ds(0, 3)], OUT_X)
    wait_send(o2.at[pl.ds(0, ng - 1)], OUT_GRP)
    wait_send(z_buf.at[pl.ds(0, ng - 1)], GRP)
    wait_send(o3.at[pl.ds(0, 7)], OUT_ZY)

    wait_recv(ga_buf.at[0, pl.ds(0, nc - 1)], ALL)
    remote(ga_buf.at[core], ga_buf.at[core], ALL_TWIN, twin).start()

    def write(side):
        for j in range(2):
            cols = pl.ds(pl.multiple_of(side * half_hid + j * bw, bw), bw)
            for i in range(nc // 2):
                gh_ref[16 * i : 16 * i + 16, cols] = ga_buf[side, 2 * i + j].astype(F32)

    write(core)
    wait_recv(o4.at[0], OUT_TWIN)
    go_ref[...] = jnp.concatenate([o4[0, 0:4], o4[1, 0:4]], axis=0)
    wait_recv(ga_buf.at[0], ALL_TWIN)
    write(1 - core)
    wait_send(ga_buf.at[0, pl.ds(0, nc - 1)], ALL)
    wait_send(ga_buf.at[0], ALL_TWIN)
    wait_send(o4.at[0], OUT_TWIN)


def write_out(logits_in, gh_in, go_in, logits_out, gh_out, go_out, sems):
    pairs = ((logits_in, logits_out), (gh_in, gh_out), (go_in, go_out))
    copies = [pltpu.make_async_copy(a, b, sems.at[i]) for i, (a, b) in enumerate(pairs)]
    for copy in copies:
        copy.start()
    for copy in copies:
        copy.wait()


def on_device(ns, ng, candidates, behav_keys, behav_values, w_query, w_hidden, w_out, clicks):
    users, per_dev, width = candidates.shape
    length = behav_keys.shape[1]
    feats, hid = w_hidden.shape
    nc = ns // 2
    hbm_spec = pl.BlockSpec(memory_space=pltpu.HBM)
    vmem_spec = pl.BlockSpec(memory_space=pltpu.VMEM)
    logits, grad_hidden, grad_out = pl.pallas_call(
        functools.partial(kernel, nc, ng),
        out_shape=(
            jax.ShapeDtypeStruct((per_dev, users), F32),
            jax.ShapeDtypeStruct((feats, hid), F32),
            jax.ShapeDtypeStruct((8, width), F32),
        ),
        in_specs=[hbm_spec] * 7,
        out_specs=(vmem_spec, vmem_spec, vmem_spec),
        scratch_shapes=[
            pltpu.VMEM((2, ns, 16, width), BF16),
            pltpu.VMEM((ns * 16, width), F32),
            pltpu.VMEM((2, ns * 16, width), F32),
            pltpu.VMEM((users, length, width), BF16),
            pltpu.VMEM((users, length, width), BF16),
            pltpu.VMEM((length, HEADS * width), F32),
            pltpu.VMEM((length, HEADS * width), F32),
            pltpu.VMEM((HEADS * width, width), BF16),
            pltpu.VMEM((width, width), BF16),
            pltpu.VMEM((feats, hid), BF16),
            pltpu.VMEM((1, hid), F32),
            pltpu.VMEM((per_dev, users), jnp.int32),
            pltpu.VMEM((per_dev, users, width), F32),
            pltpu.VMEM((2, width, width), F32),
            pltpu.VMEM((users - DIRECT, 2, 2, 64, width), F32),
            pltpu.VMEM((users - DIRECT, 2, 64, width), F32),
            pltpu.VMEM((nc + 2 * DIRECT, 40, width), F32),
            pltpu.VMEM((nc + 2 * DIRECT, 40, width), F32),
            pltpu.VMEM((64, width), F32),
            pltpu.VMEM((64, width), F32),
            pltpu.VMEM((nc, 16, hid // 4), BF16),
            pltpu.VMEM((nc, 16, hid // 4), BF16),
            pltpu.VMEM((ng, 16, hid // 4), F32),
            pltpu.VMEM((2, nc, 16, hid // 4), BF16),
            pltpu.VMEM((nc, 1, width), F32),
            pltpu.VMEM((nc, 1, width), F32),
            pltpu.VMEM((4, 8, width), F32),
            pltpu.VMEM((ng, 8, width), F32),
            pltpu.VMEM((8, 8, width), F32),
            pltpu.VMEM((2, 8, width), F32),
            pltpu.SemaphoreType.DMA((2, users)),
            pltpu.SemaphoreType.DMA((6,)),
            pltpu.SemaphoreType.DMA((users - DIRECT,)),
            pltpu.SemaphoreType.DMA,
            pltpu.SemaphoreType.DMA((PHASES,)),
            pltpu.SemaphoreType.DMA((PHASES,)),
        ],
        compiler_params=pltpu.CompilerParams(
            collective_id=0, has_side_effects=True, vmem_limit_bytes=40 * 2**20
        ),
        name="ranker",
    )(
        *(
            pltpu.with_memory_space_constraint(operand, pltpu.HBM)
            for operand in (
                candidates.reshape(users * per_dev, width),
                behav_keys,
                behav_values,
                w_query,
                w_hidden,
                w_out.reshape(1, hid),
                jnp.transpose(clicks),
            )
        )
    )
    results = (logits, grad_hidden, grad_out)
    logits, grad_hidden, grad_out = pl.pallas_call(
        write_out,
        out_shape=[jax.ShapeDtypeStruct(r.shape, r.dtype) for r in results],
        in_specs=[vmem_spec] * 3,
        out_specs=[hbm_spec] * 3,
        scratch_shapes=[pltpu.SemaphoreType.DMA((3,))],
        name="write_out",
    )(*results)
    return jnp.transpose(logits), grad_hidden, grad_out.reshape(hid)


def solution(mesh):
    return jax.shard_map(
        functools.partial(on_device, mesh.shape["seq"], mesh.shape["grp"]),
        mesh=mesh,
        in_specs=(
            P("grp", "seq", None),
            P("grp", "seq", None),
            P("grp", "seq", None),
            P(),
            P(),
            P(),
            P("grp", "seq"),
        ),
        out_specs=(P("grp", "seq"), P(), P()),
        check_vma=False,
    )
```

```python
import functools
import math

import jax
import jax.numpy as jnp
from jax import lax
from jax.experimental import pallas as pl
from jax.experimental.pallas import tpu as pltpu
from jax.sharding import PartitionSpec as P

HEADS = 4
MESH = pl.DeviceIdType.MESH
NT = (((1,), (1,)), ((), ()))
F32 = jnp.float32
BF16 = jnp.bfloat16
GATHER, GATHER_TWIN, PARTIAL, TWIN_HEAD, OUT_X, LOGITS, OUT_GRP, OUT_ZY, OUT_TWIN = 0, 2, 4, 5, 6, 7, 8, 9, 10
REDUCE, GRP, ALL, ALL_TWIN = 11, 13, 15, 17
PHASES = 19
CHUNK = 512


def kernel(
    nc,
    ng,
    cand_hbm,
    keys_hbm,
    vals_hbm,
    wq_hbm,
    wh_hbm,
    wout_hbm,
    clicks_hbm,
    logits_ref,
    gh_ref,
    go_ref,
    x_buf,
    xf,
    qf,
    k_buf,
    v_buf,
    s_even,
    s_odd,
    q_heads,
    wq_buf,
    wh_buf,
    wout_ref,
    clicks_ref,
    clk,
    mine,
    theirs,
    p_send,
    p_recv,
    h_send,
    h_recv,
    g_send,
    g_recv,
    z_buf,
    ga_buf,
    l_send,
    l_recv,
    o1,
    o2,
    o3,
    o4,
    kv_sems,
    w_sems,
    twin_sems,
    twin_send_sem,
    send_sems,
    recv_sems,
):
    me = lax.axis_index("seq")
    grp = lax.axis_index("grp")
    core = lax.rem(me, 2)
    chip = me // 2
    users, length, width = k_buf.shape
    half_users = users // 2
    u_me = me // 4
    c_me = lax.rem(chip, 2)
    first_half = 1 - u_me // half_users
    head_size = width // HEADS
    scale = math.log2(math.e) / math.sqrt(head_size)
    hw = HEADS * width

    def user_at(t):
        return lax.rem(first_half + t // half_users, 2) * half_users + lax.rem(
            u_me + 1 + t, half_users
        )

    def on_chip(k):
        return lax.rem(chip + k, nc)

    def remote(src, dst, phase, seq, group=None):
        where = {"seq": seq} if group is None else {"seq": seq, "grp": group}
        return pltpu.make_async_remote_copy(
            src_ref=src,
            dst_ref=dst,
            send_sem=send_sems.at[phase],
            recv_sem=recv_sems.at[phase],
            device_id=where,
            device_id_type=MESH,
        )

    twin = chip * 2 + 1 - core

    def same_core(other_chip):
        return other_chip * 2 + core

    def local(src, dst, sem):
        return pltpu.make_async_copy(src, dst, sem)

    def wait_send(ref, phase):
        local(ref, ref, send_sems.at[phase]).wait()

    def wait_recv(ref, phase):
        local(ref, ref, recv_sems.at[phase]).wait()

    own_loads = [
        local(cand_hbm.at[pl.ds(16 * i, 16)], x_buf.at[i, core * nc + chip], w_sems.at[i])
        for i in range(2)
    ]
    for load in own_loads:
        load.start()
    wq_load = local(wq_hbm, wq_buf, w_sems.at[2])
    wq_load.start()
    clicks_load = local(clicks_hbm, clicks_ref, w_sems.at[4])
    clicks_load.start()

    @pl.loop(0, users)
    def _(t):
        u = user_at(t)
        local(keys_hbm.at[u], k_buf.at[u], kv_sems.at[0, t]).start()
        local(vals_hbm.at[u], v_buf.at[u], kv_sems.at[1, t]).start()

    wh_load = local(wh_hbm, wh_buf, w_sems.at[3])
    wh_load.start()
    wout_load = local(wout_hbm, wout_ref, w_sems.at[5])
    wout_load.start()

    barrier = pltpu.get_barrier_semaphore()
    pl.semaphore_signal(barrier, inc=1, device_id={"seq": twin}, device_id_type=MESH)

    @pl.loop(1, nc)
    def _(k):
        pl.semaphore_signal(
            barrier, inc=1, device_id={"seq": same_core(on_chip(k))}, device_id_type=MESH
        )

    for k in range(1, ng):
        pl.semaphore_signal(
            barrier,
            inc=1,
            device_id={"seq": me, "grp": lax.rem(grp + k, ng)},
            device_id_type=MESH,
        )

    clicks_load.wait()
    row_u = lax.broadcasted_iota(jnp.int32, (users, users), 0)
    col_u = lax.broadcasted_iota(jnp.int32, (users, users), 1)
    for c in range(2):
        wide = jnp.broadcast_to(clicks_ref[c : c + 1, :].astype(F32), (users, users))
        column = jnp.sum(jnp.where(row_u == col_u, wide, 0.0), axis=1, keepdims=True)
        clk[c] = jnp.broadcast_to(column, (users, width))

    pl.semaphore_wait(barrier, nc + ng - 1)

    for load in own_loads:
        load.wait()
    own = core * nc + chip

    def send_candidates(turn):
        @pl.loop(1, nc)
        def _(k):
            to = on_chip(k)
            part = lax.rem(to // (nc // 2) + 1 + turn, 2)
            remote(
                x_buf.at[part, own], x_buf.at[part, own], GATHER + part, same_core(to)
            ).start()

    send_candidates(0)

    def pass_on(part):
        wait_recv(x_buf.at[0, pl.ds(0, nc - 1)], GATHER + part)
        block = x_buf.at[part, pl.ds(core * nc, nc)]
        remote(block, block, GATHER_TWIN + part, twin).start()

    def make_queries(part):
        wait_recv(x_buf.at[0, pl.ds(0, nc)], GATHER_TWIN + part)
        x_all = x_buf[part].reshape(2 * nc * 16, width)
        queries = jnp.dot(x_all, wq_buf[...], preferred_element_type=F32)
        qf[part] = queries.astype(BF16).astype(F32)

    second_half = 1 - first_half
    wq_load.wait()
    pass_on(first_half)
    send_candidates(1)
    make_queries(first_half)

    head_of = lax.broadcasted_iota(jnp.int32, (2 * nc, width), 1) // head_size
    lane8 = lax.broadcasted_iota(jnp.int32, (8, width), 1)
    row8 = lax.broadcasted_iota(jnp.int32, (8, width), 0)
    group8 = lax.rem(lane8, head_size) // 8
    is_lse = lax.rem(lane8, 8) == 0
    is_click = lax.rem(lane8, 8) == 1
    at_me = (row8 == lax.rem(chip, 8)) & (group8 == chip // 8) & is_click

    def set_queries(u):
        part = u // half_users
        for c in range(2):
            rows = qf[part, pl.ds(lax.rem(u, half_users) * 2 + c, 2 * nc, stride=16), :]
            for h in range(HEADS):
                first = h * width + c * 2 * nc
                q_heads[first : first + 2 * nc, :] = jnp.where(head_of == h, rows, 0.0).astype(
                    BF16
                )

    def scores(u, j, s_ref, highest):
        rows = slice(j * CHUNK, j * CHUNK + CHUNK)
        s = lax.dot_general(k_buf[u, rows, :], q_heads[...], NT, preferred_element_type=F32)
        s_ref[rows, :] = s
        return jnp.maximum(highest, jnp.max(s.reshape(CHUNK // 8, 8, hw), axis=0))

    lowest = jnp.full((8, hw), -jnp.inf, F32)

    def attend(t, s_ref, s_next, highest, more=True):
        u = user_at(t)
        top = jnp.max(highest, axis=0, keepdims=True) * scale
        local(vals_hbm.at[u], v_buf.at[u], kv_sems.at[1, t]).wait()
        vals = jnp.transpose(v_buf[u])
        if more:
            u_next = user_at(t + 1)
            local(keys_hbm.at[u_next], k_buf.at[u_next], kv_sems.at[0, t + 1]).wait()
            set_queries(u_next)
        highest = lowest
        den = jnp.zeros((8, hw), F32)
        num = [jnp.zeros((2 * head_size, 2 * width), F32) for _ in range(HEADS // 2)]
        for j in range(length // CHUNK):
            if more:
                highest = scores(u_next, j, s_next, highest)
            rows = slice(j * CHUNK, j * CHUNK + CHUNK)
            p = jnp.exp2(s_ref[rows, :] * scale - top)
            den = den + jnp.sum(p.reshape(CHUNK // 8, 8, hw), axis=0)
            probs = p.astype(BF16)
            for h in range(HEADS // 2):
                num[h] = num[h] + jnp.dot(
                    vals[2 * head_size * h : 2 * head_size * (h + 1), rows],
                    probs[:, 2 * width * h : 2 * width * (h + 1)],
                    preferred_element_type=F32,
                )
        den = jnp.sum(den, axis=0, keepdims=True)
        inverse = 1.0 / den
        lse = top + jnp.log2(den)
        att_rows, lse_rows = [], []
        for h in range(HEADS):
            cols = slice(width * h, width * (h + 1))
            sub, at = head_size * (h % 2), width * (h % 2)
            block = num[h // 2][sub : sub + head_size, at : at + width]
            att_rows.append(block * inverse[:, cols])
            lse_rows.append(jnp.broadcast_to(lse[:, cols], (head_size, width)))
        att = jnp.transpose(jnp.concatenate(att_rows, axis=0))
        lse = jnp.transpose(jnp.concatenate(lse_rows, axis=0))
        for c in range(2):
            for half in range(2):
                first = 64 * c + 32 * half
                mine[t, half, c, 0:32] = att[first : first + 32]
                mine[t, half, c, 32:64] = lse[first : first + 32]
        pltpu.make_async_remote_copy(
            src_ref=mine.at[t, 1 - core],
            dst_ref=theirs.at[t],
            send_sem=twin_send_sem,
            recv_sem=twin_sems.at[t],
            device_id={"seq": twin},
            device_id_type=MESH,
        ).start()
        return highest

    def merge(t):
        u = user_at(t)
        local(theirs.at[t], theirs.at[t], twin_sems.at[t]).wait()
        for c in range(2):
            a, b = mine[t, core, c], theirs[t, c]
            top = jnp.maximum(a[32:64], b[32:64])
            wa, wb = jnp.exp2(a[32:64] - top), jnp.exp2(b[32:64] - top)
            total = wa + wb
            lse = top + jnp.log2(total)
            slot = t * 2 + c
            p_send[slot, 0:32] = (a[0:32] * wa + b[0:32] * wb) / total
            tile = jnp.zeros((8, width), F32)
            for g in range(4):
                tile = jnp.where(is_lse & (group8 == g), lse[8 * g : 8 * g + 8], tile)
            click = jnp.broadcast_to(clk[c, pl.ds(u, 1), :], (8, width))
            p_send[slot, 32:40] = jnp.where(at_me, click, tile)
            to = 4 * u + 2 * c + core

            @pl.when(to != me)
            def _():
                remote(p_send.at[slot], p_recv.at[chip], PARTIAL, to).start()

            @pl.when(to == me)
            def _():
                local(p_send.at[slot], p_recv.at[chip], recv_sems.at[PARTIAL]).start()

    u_first = user_at(0)
    local(keys_hbm.at[u_first], k_buf.at[u_first], kv_sems.at[0, 0]).wait()
    set_queries(u_first)
    highest = lowest
    for j in range(length // CHUNK):
        highest = scores(u_first, j, s_even, highest)

    def two_users(i, highest):
        t = 2 * i

        @pl.when(i == half_users // 2 - 1)
        def _():
            pass_on(second_half)

        highest = attend(t, s_even, s_odd, highest)

        @pl.when(i > 0)
        def _():
            merge(t - 1)

        @pl.when(i == half_users // 2 - 1)
        def _():
            make_queries(second_half)
            xf[...] = x_buf[second_half].reshape(2 * nc * 16, width).astype(F32)

        highest = attend(t + 1, s_odd, s_even, highest)
        merge(t)
        return highest

    highest = lax.fori_loop(0, users // 2 - 1, two_users, highest)
    highest = attend(users - 2, s_even, s_odd, highest)
    merge(users - 3)
    attend(users - 1, s_odd, None, highest, more=False)
    merge(users - 2)
    merge(users - 1)

    wait_recv(p_recv, PARTIAL)
    ej = lax.broadcasted_iota(jnp.int32, (width, 4 * width), 0)
    ef = lax.broadcasted_iota(jnp.int32, (width, 4 * width), 1)
    same = (ej // head_size == lax.rem(ef, width) // head_size) & (
        lax.rem(ej, head_size) // 8 == ef // width
    )
    spread = jnp.where(same & (lax.rem(ej, 8) == 0), 1.0, 0.0).astype(BF16)
    spread_click = jnp.where(same & (lax.rem(ej, 8) == 1), 1.0, 0.0).astype(BF16)
    tiles = p_recv[:, 32:40, :]
    rest = tiles.reshape(nc * 8, width)
    lse_all = jnp.zeros((nc * 8, 4 * width), F32)
    for _ in range(3):
        piece = rest.astype(BF16)
        rest = rest - piece.astype(F32)
        lse_all = lse_all + jnp.dot(piece, spread, preferred_element_type=F32)
    lse_all = lse_all.reshape(nc, 8, 4 * width)
    w = jnp.exp2(lse_all - jnp.max(lse_all, axis=0)[None])
    den = jnp.sum(w, axis=0)
    attended = []
    for g in range(4):
        cols = slice(g * width, g * width + width)
        num = jnp.sum(p_recv[:, 8 * g : 8 * g + 8, :] * w[:, :, cols], axis=0)
        attended.append(num / den[:, cols])
    attended = jnp.concatenate(attended, axis=0).astype(BF16).astype(F32)
    click_tile = jnp.where(is_click, jnp.sum(tiles, axis=0), 0.0)
    click = jnp.dot(click_tile.astype(BF16), spread_click, preferred_element_type=F32)
    click = jnp.concatenate([click[:, g * width : g * width + width] for g in range(4)], axis=0)
    click = click[:, 0:1]

    def candidates_of(which):
        first = which * nc * 16 + lax.rem(u_me, half_users) * 2 + c_me
        return xf[pl.ds(first, nc, stride=16), :]

    features = jnp.concatenate([candidates_of(core), attended], axis=1)
    wh_load.wait()
    wout_load.wait()
    pre = jnp.dot(features.astype(BF16), wh_buf[...], preferred_element_type=F32)
    hidden = jnp.maximum(pre, 0.0).astype(BF16).astype(F32)
    logits = jnp.sum(hidden * wout_ref[...], axis=-1, keepdims=True)
    dlogit = 1.0 / (1.0 + jnp.exp(-logits)) - click
    h_send[0:32] = attended
    h_send[32:64] = jnp.broadcast_to(dlogit, (nc, width))
    remote(h_send, h_recv, TWIN_HEAD, twin).start()

    half_hid = wh_buf.shape[1] // 2
    my_cols = pl.ds(pl.multiple_of(core * half_hid, half_hid), half_hid)
    wout = wout_ref[:, my_cols]

    def half_of(a):
        return jnp.where(core == 0, a[:, :half_hid], a[:, half_hid:])

    def dpre_of(pre, dlogit):
        return jnp.where(pre > 0.0, dlogit * wout, 0.0).astype(BF16)

    dpre = dpre_of(half_of(pre), dlogit)
    out_part = jnp.sum(half_of(hidden) * dlogit, axis=0, keepdims=True)
    wait_recv(h_recv, TWIN_HEAD)
    other = jnp.concatenate([candidates_of(1 - core), h_recv[0:32]], axis=1)
    dlogit = h_recv[32:64, 0:1]
    pre = jnp.dot(other.astype(BF16), wh_buf[:, my_cols], preferred_element_type=F32)
    hidden = jnp.maximum(pre, 0.0).astype(BF16).astype(F32)
    out_part = out_part + jnp.sum(hidden * dlogit, axis=0, keepdims=True)
    features = jnp.concatenate([features, other], axis=0)
    dpre = jnp.concatenate([dpre, dpre_of(pre, dlogit)], axis=0)
    grad = jnp.dot(jnp.transpose(features).astype(BF16), dpre, preferred_element_type=F32)
    bw = half_hid // 2
    for part in range(2):
        for b in range(nc):
            i, j = b // 2, b % 2
            first = bw * j + width * part
            g_send[part, b] = grad[16 * i : 16 * i + 16, first : first + width].astype(BF16)

        @pl.loop(1, nc)
        def _(k):
            to = on_chip(k)
            remote(
                g_send.at[part, to], g_recv.at[part, chip], REDUCE + part, same_core(to)
            ).start()

        g_recv[part, chip] = g_send[part, chip]

    at_x, at_zy = lax.rem(chip, 4), chip // 4
    pieces = [out_part[:, width * i : width * i + width] for i in range(4)]
    o1[at_x] = jnp.concatenate(pieces + [jnp.zeros((4, width), F32)], axis=0)
    for k in range(1, 4):
        to = at_zy * 4 + lax.rem(at_x + k, 4)
        remote(o1.at[at_x], o1.at[at_x], OUT_X, same_core(to)).start()

    wide = jnp.broadcast_to(logits, (nc, width))
    for i in range(nc):
        l_send[i] = wide[i : i + 1, :]
    l_slot = c_me * users + u_me

    @pl.loop(1, nc)
    def _(k):
        to = on_chip(k)
        remote(l_send.at[to], l_recv.at[l_slot], LOGITS, same_core(to)).start()

    l_recv[l_slot] = l_send[chip]

    wait_recv(o1.at[pl.ds(0, 3)], OUT_X)
    o2[grp] = o1[0] + o1[1] + o1[2] + o1[3]
    for k in range(1, ng):
        remote(o2.at[grp], o2.at[grp], OUT_GRP, me, lax.rem(grp + k, ng)).start()
    for part in range(2):
        wait_recv(g_recv.at[part, pl.ds(0, nc - 1)], REDUCE + part)
        z_buf[part, grp] = jnp.sum(g_recv[part].astype(F32), axis=0).astype(BF16)
        for k in range(1, ng):
            block = z_buf.at[part, grp]
            remote(block, block, GRP + part, me, lax.rem(grp + k, ng)).start()
    wait_recv(o2.at[pl.ds(0, ng - 1)], OUT_GRP)
    o3[at_zy] = jnp.sum(o2[...], axis=0)
    for k in range(1, 8):
        to = lax.rem(at_zy + k, 8) * 4 + at_x
        remote(o3.at[at_zy], o3.at[at_zy], OUT_ZY, same_core(to)).start()
    for part in range(2):
        wait_recv(z_buf.at[part, pl.ds(0, ng - 1)], GRP + part)
        ga_buf[part, core, chip] = jnp.sum(z_buf[part].astype(F32), axis=0).astype(BF16)

        @pl.loop(1, nc)
        def _(k):
            block = ga_buf.at[part, core, chip]
            remote(block, block, ALL + part, same_core(on_chip(k))).start()

    wait_recv(l_recv.at[pl.ds(0, nc - 1)], LOGITS)
    logit_rows = l_recv[...].reshape(2 * users, width)
    row_o = lax.broadcasted_iota(jnp.int32, (users, width), 0)
    col_o = lax.broadcasted_iota(jnp.int32, (users, width), 1)
    for c in range(2):
        rows = jnp.where(row_o == col_o, logit_rows[users * c : users * (c + 1)], 0.0)
        logits_ref[c : c + 1, :] = jnp.sum(rows, axis=0, keepdims=True)[:, :users]
    wait_recv(o3.at[pl.ds(0, 7)], OUT_ZY)
    o4[core] = jnp.sum(o3[...], axis=0)
    remote(o4.at[core], o4.at[core], OUT_TWIN, twin).start()

    for part in range(2):
        wait_send(x_buf.at[0, pl.ds(0, nc - 1)], GATHER + part)
        wait_send(x_buf.at[0, pl.ds(0, nc)], GATHER_TWIN + part)
    local(theirs, theirs, twin_send_sem).wait()
    wait_send(p_send.at[pl.ds(0, nc - 1)], PARTIAL)
    wait_send(h_send, TWIN_HEAD)
    wait_send(l_send.at[pl.ds(0, nc - 1)], LOGITS)
    for part in range(2):
        wait_send(g_send.at[part, pl.ds(0, nc - 1)], REDUCE + part)
        wait_send(z_buf.at[part, pl.ds(0, ng - 1)], GRP + part)
    wait_send(o1.at[pl.ds(0, 3)], OUT_X)
    wait_send(o2.at[pl.ds(0, ng - 1)], OUT_GRP)
    wait_send(o3.at[pl.ds(0, 7)], OUT_ZY)

    def write(part, side):
        for j in range(2):
            first = side * half_hid + j * bw + part * width
            cols = pl.ds(pl.multiple_of(first, width), width)
            for i in range(nc // 2):
                gh_ref[16 * i : 16 * i + 16, cols] = ga_buf[part, side, 2 * i + j].astype(F32)

    for part in range(2):
        wait_recv(ga_buf.at[part, 0, pl.ds(0, nc - 1)], ALL + part)
        block = ga_buf.at[part, core]
        remote(block, block, ALL_TWIN + part, twin).start()
        write(part, core)
    wait_recv(o4.at[0], OUT_TWIN)
    go_ref[...] = jnp.concatenate([o4[0, 0:4], o4[1, 0:4]], axis=0)
    for part in range(2):
        wait_recv(ga_buf.at[part, 0], ALL_TWIN + part)
        write(part, 1 - core)
    for part in range(2):
        wait_send(ga_buf.at[part, 0, pl.ds(0, nc - 1)], ALL + part)
        wait_send(ga_buf.at[part, 0], ALL_TWIN + part)
    wait_send(o4.at[0], OUT_TWIN)


def on_device(ns, ng, candidates, behav_keys, behav_values, w_query, w_hidden, w_out, clicks):
    users, per_dev, width = candidates.shape
    length = behav_keys.shape[1]
    feats, hid = w_hidden.shape
    nc = ns // 2
    hbm_spec = pl.BlockSpec(memory_space=pltpu.HBM)
    vmem_spec = pl.BlockSpec(memory_space=pltpu.VMEM)
    logits, grad_hidden, grad_out = pl.pallas_call(
        functools.partial(kernel, nc, ng),
        out_shape=(
            jax.ShapeDtypeStruct((per_dev, users), F32),
            jax.ShapeDtypeStruct((feats, hid), F32),
            jax.ShapeDtypeStruct((8, width), F32),
        ),
        in_specs=[hbm_spec] * 7,
        out_specs=(vmem_spec, vmem_spec, vmem_spec),
        scratch_shapes=[
            pltpu.VMEM((2, ns, 16, width), BF16),
            pltpu.VMEM((ns * 16, width), F32),
            pltpu.VMEM((2, ns * 16, width), F32),
            pltpu.VMEM((users, length, width), BF16),
            pltpu.VMEM((users, length, width), BF16),
            pltpu.VMEM((length, HEADS * width), F32),
            pltpu.VMEM((length, HEADS * width), F32),
            pltpu.VMEM((HEADS * width, width), BF16),
            pltpu.VMEM((width, width), BF16),
            pltpu.VMEM((feats, hid), BF16),
            pltpu.VMEM((1, hid), F32),
            pltpu.VMEM((per_dev, users), jnp.int32),
            pltpu.VMEM((per_dev, users, width), F32),
            pltpu.VMEM((users, 2, 2, 64, width), F32),
            pltpu.VMEM((users, 2, 64, width), F32),
            pltpu.VMEM((nc, 40, width), F32),
            pltpu.VMEM((nc, 40, width), F32),
            pltpu.VMEM((64, width), F32),
            pltpu.VMEM((64, width), F32),
            pltpu.VMEM((2, nc, 16, width), BF16),
            pltpu.VMEM((2, nc, 16, width), BF16),
            pltpu.VMEM((2, ng, 16, width), BF16),
            pltpu.VMEM((2, 2, nc, 16, width), BF16),
            pltpu.VMEM((nc, 1, width), F32),
            pltpu.VMEM((nc, 1, width), F32),
            pltpu.VMEM((4, 8, width), F32),
            pltpu.VMEM((ng, 8, width), F32),
            pltpu.VMEM((8, 8, width), F32),
            pltpu.VMEM((2, 8, width), F32),
            pltpu.SemaphoreType.DMA((2, users)),
            pltpu.SemaphoreType.DMA((6,)),
            pltpu.SemaphoreType.DMA((users,)),
            pltpu.SemaphoreType.DMA,
            pltpu.SemaphoreType.DMA((PHASES,)),
            pltpu.SemaphoreType.DMA((PHASES,)),
        ],
        compiler_params=pltpu.CompilerParams(
            collective_id=0, has_side_effects=True, vmem_limit_bytes=40 * 2**20
        ),
        name="ranker",
    )(
        *(
            pltpu.with_memory_space_constraint(operand, pltpu.HBM)
            for operand in (
                candidates.reshape(users * per_dev, width),
                behav_keys,
                behav_values,
                w_query,
                w_hidden,
                w_out.reshape(1, hid),
                jnp.transpose(clicks),
            )
        )
    )
    return jnp.transpose(logits), grad_hidden, grad_out.reshape(hid)


def solution(mesh):
    return jax.shard_map(
        functools.partial(on_device, mesh.shape["seq"], mesh.shape["grp"]),
        mesh=mesh,
        in_specs=(
            P("grp", "seq", None),
            P("grp", "seq", None),
            P("grp", "seq", None),
            P(),
            P(),
            P(),
            P("grp", "seq"),
        ),
        out_specs=(P("grp", "seq"), P(), P()),
        check_vma=False,
    )
```

```python
import functools
import math

import jax
import jax.numpy as jnp
from jax import lax
from jax.experimental import pallas as pl
from jax.experimental.pallas import tpu as pltpu
from jax.sharding import PartitionSpec as P

HEADS = 4
MESH = pl.DeviceIdType.MESH
NT = (((1,), (1,)), ((), ()))
F32 = jnp.float32
BF16 = jnp.bfloat16
GATHER, GATHER_TWIN, PARTIAL, TWIN_HEAD, OUT_X, LOGITS, OUT_GRP, OUT_ZY, OUT_TWIN = 0, 2, 4, 5, 6, 7, 8, 9, 10
REDUCE, GRP, ALL, ALL_TWIN = 11, 13, 15, 17
PHASES = 19
CHUNK = 512


def kernel(
    nc,
    ng,
    cand_hbm,
    keys_hbm,
    vals_hbm,
    wq_hbm,
    wh_hbm,
    wout_hbm,
    clicks_hbm,
    logits_ref,
    gh_ref,
    go_ref,
    x_buf,
    xf,
    qf,
    k_buf,
    v_buf,
    s_even,
    s_odd,
    q_heads,
    wq_buf,
    wh_buf,
    wout_ref,
    clicks_ref,
    clk,
    mine,
    theirs,
    p_send,
    p_recv,
    h_send,
    h_recv,
    g_send,
    g_recv,
    z_buf,
    ga_buf,
    l_send,
    l_recv,
    o1,
    o2,
    o3,
    o4,
    kv_sems,
    w_sems,
    twin_sems,
    twin_send_sem,
    send_sems,
    recv_sems,
):
    me = lax.axis_index("seq")
    grp = lax.axis_index("grp")
    core = lax.rem(me, 2)
    chip = me // 2
    users, length, width = k_buf.shape
    half_users = users // 2
    u_me = me // 4
    c_me = lax.rem(chip, 2)
    first_half = 1 - u_me // half_users
    head_size = width // HEADS
    scale = math.log2(math.e) / math.sqrt(head_size)
    hw = HEADS * width

    def user_at(t):
        turn = lax.rem(t, half_users)
        offset = 0
        for place, step in enumerate((4, 3, 5, 1, 7, 2, 6, 0)):
            offset = jnp.where(turn == place, step, offset)
        return lax.rem(first_half + t // half_users, 2) * half_users + lax.rem(
            u_me + offset, half_users
        )

    def on_chip(k):
        return lax.rem(chip + k, nc)

    def remote(src, dst, phase, seq, group=None):
        where = {"seq": seq} if group is None else {"seq": seq, "grp": group}
        return pltpu.make_async_remote_copy(
            src_ref=src,
            dst_ref=dst,
            send_sem=send_sems.at[phase],
            recv_sem=recv_sems.at[phase],
            device_id=where,
            device_id_type=MESH,
        )

    twin = chip * 2 + 1 - core

    def same_core(other_chip):
        return other_chip * 2 + core

    def local(src, dst, sem):
        return pltpu.make_async_copy(src, dst, sem)

    def wait_send(ref, phase):
        local(ref, ref, send_sems.at[phase]).wait()

    def wait_recv(ref, phase):
        local(ref, ref, recv_sems.at[phase]).wait()

    barrier = pltpu.get_barrier_semaphore()
    pl.semaphore_signal(barrier, inc=1, device_id={"seq": twin}, device_id_type=MESH)

    @pl.loop(1, nc)
    def _(k):
        pl.semaphore_signal(
            barrier, inc=1, device_id={"seq": same_core(on_chip(k))}, device_id_type=MESH
        )

    for k in range(1, ng):
        pl.semaphore_signal(
            barrier,
            inc=1,
            device_id={"seq": me, "grp": lax.rem(grp + k, ng)},
            device_id_type=MESH,
        )

    own_loads = [
        local(cand_hbm.at[pl.ds(16 * i, 16)], x_buf.at[i, core * nc + chip], w_sems.at[i])
        for i in range(2)
    ]
    for load in own_loads:
        load.start()
    wq_load = local(wq_hbm, wq_buf, w_sems.at[2])
    wq_load.start()
    clicks_load = local(clicks_hbm, clicks_ref, w_sems.at[4])
    clicks_load.start()

    @pl.loop(0, users)
    def _(t):
        u = user_at(t)
        local(keys_hbm.at[u], k_buf.at[u], kv_sems.at[0, t]).start()
        local(vals_hbm.at[u], v_buf.at[u], kv_sems.at[1, t]).start()

    wh_load = local(wh_hbm, wh_buf, w_sems.at[3])
    wh_load.start()
    wout_load = local(wout_hbm, wout_ref, w_sems.at[5])
    wout_load.start()

    clicks_load.wait()
    row_u = lax.broadcasted_iota(jnp.int32, (users, users), 0)
    col_u = lax.broadcasted_iota(jnp.int32, (users, users), 1)
    for c in range(2):
        wide = jnp.broadcast_to(clicks_ref[c : c + 1, :].astype(F32), (users, users))
        column = jnp.sum(jnp.where(row_u == col_u, wide, 0.0), axis=1, keepdims=True)
        clk[c] = jnp.broadcast_to(column, (users, width))

    pl.semaphore_wait(barrier, nc + ng - 1)

    for load in own_loads:
        load.wait()
    own = core * nc + chip

    def send_candidates(turn):
        @pl.loop(1, nc)
        def _(k):
            to = on_chip(k)
            part = lax.rem(to // (nc // 2) + 1 + turn, 2)
            remote(
                x_buf.at[part, own], x_buf.at[part, own], GATHER + part, same_core(to)
            ).start()

    send_candidates(0)

    def pass_on(part):
        wait_recv(x_buf.at[0, pl.ds(0, nc - 1)], GATHER + part)
        block = x_buf.at[part, pl.ds(core * nc, nc)]
        remote(block, block, GATHER_TWIN + part, twin).start()

    def make_queries(part):
        wait_recv(x_buf.at[0, pl.ds(0, nc)], GATHER_TWIN + part)
        x_all = x_buf[part].reshape(2 * nc * 16, width)
        queries = jnp.dot(x_all, wq_buf[...], preferred_element_type=F32)
        qf[part] = queries.astype(BF16).astype(F32)

    second_half = 1 - first_half
    wq_load.wait()
    pass_on(first_half)
    send_candidates(1)
    make_queries(first_half)

    head_of = lax.broadcasted_iota(jnp.int32, (2 * nc, width), 1) // head_size
    lane8 = lax.broadcasted_iota(jnp.int32, (8, width), 1)
    row8 = lax.broadcasted_iota(jnp.int32, (8, width), 0)
    group8 = lax.rem(lane8, head_size) // 8
    is_lse = lax.rem(lane8, 8) == 0
    is_click = lax.rem(lane8, 8) == 1
    at_me = (row8 == lax.rem(chip, 8)) & (group8 == chip // 8) & is_click

    def set_queries(u):
        part = u // half_users
        for c in range(2):
            rows = qf[part, pl.ds(lax.rem(u, half_users) * 2 + c, 2 * nc, stride=16), :]
            for h in range(HEADS):
                first = h * width + c * 2 * nc
                q_heads[first : first + 2 * nc, :] = jnp.where(head_of == h, rows, 0.0).astype(
                    BF16
                )

    def scores(u, j, s_ref, highest):
        rows = slice(j * CHUNK, j * CHUNK + CHUNK)
        s = lax.dot_general(k_buf[u, rows, :], q_heads[...], NT, preferred_element_type=F32)
        s_ref[rows, :] = s
        return jnp.maximum(highest, jnp.max(s.reshape(CHUNK // 8, 8, hw), axis=0))

    lowest = jnp.full((8, hw), -jnp.inf, F32)

    def attend(t, s_ref, s_next, highest, more=True):
        u = user_at(t)
        top = jnp.max(highest, axis=0, keepdims=True) * scale
        local(vals_hbm.at[u], v_buf.at[u], kv_sems.at[1, t]).wait()
        vals = jnp.transpose(v_buf[u])
        if more:
            u_next = user_at(t + 1)
            local(keys_hbm.at[u_next], k_buf.at[u_next], kv_sems.at[0, t + 1]).wait()
            set_queries(u_next)
        highest = lowest
        den = jnp.zeros((8, hw), F32)
        num = [jnp.zeros((2 * head_size, 2 * width), F32) for _ in range(HEADS // 2)]
        for j in range(length // CHUNK):
            if more:
                highest = scores(u_next, j, s_next, highest)
            rows = slice(j * CHUNK, j * CHUNK + CHUNK)
            p = jnp.exp2(s_ref[rows, :] * scale - top)
            den = den + jnp.sum(p.reshape(CHUNK // 8, 8, hw), axis=0)
            probs = p.astype(BF16)
            for h in range(HEADS // 2):
                num[h] = num[h] + jnp.dot(
                    vals[2 * head_size * h : 2 * head_size * (h + 1), rows],
                    probs[:, 2 * width * h : 2 * width * (h + 1)],
                    preferred_element_type=F32,
                )
        den = jnp.sum(den, axis=0, keepdims=True)
        inverse = 1.0 / den
        lse = top + jnp.log2(den)
        att_rows, lse_rows = [], []
        for h in range(HEADS):
            cols = slice(width * h, width * (h + 1))
            sub, at = head_size * (h % 2), width * (h % 2)
            block = num[h // 2][sub : sub + head_size, at : at + width]
            att_rows.append(block * inverse[:, cols])
            lse_rows.append(jnp.broadcast_to(lse[:, cols], (head_size, width)))
        att = jnp.transpose(jnp.concatenate(att_rows, axis=0))
        lse = jnp.transpose(jnp.concatenate(lse_rows, axis=0))
        for c in range(2):
            for half in range(2):
                first = 64 * c + 32 * half
                mine[t, half, c, 0:32] = att[first : first + 32]
                mine[t, half, c, 32:64] = lse[first : first + 32]
        pltpu.make_async_remote_copy(
            src_ref=mine.at[t, 1 - core],
            dst_ref=theirs.at[t],
            send_sem=twin_send_sem,
            recv_sem=twin_sems.at[t],
            device_id={"seq": twin},
            device_id_type=MESH,
        ).start()
        return highest

    def merge(t):
        u = user_at(t)
        local(theirs.at[t], theirs.at[t], twin_sems.at[t]).wait()
        for c in range(2):
            a, b = mine[t, core, c], theirs[t, c]
            top = jnp.maximum(a[32:64], b[32:64])
            wa, wb = jnp.exp2(a[32:64] - top), jnp.exp2(b[32:64] - top)
            total = wa + wb
            lse = top + jnp.log2(total)
            slot = t * 2 + c
            p_send[slot, 0:32] = (a[0:32] * wa + b[0:32] * wb) / total
            tile = jnp.zeros((8, width), F32)
            for g in range(4):
                tile = jnp.where(is_lse & (group8 == g), lse[8 * g : 8 * g + 8], tile)
            click = jnp.broadcast_to(clk[c, pl.ds(u, 1), :], (8, width))
            p_send[slot, 32:40] = jnp.where(at_me, click, tile)
            to = 4 * u + 2 * c + core

            @pl.when(to != me)
            def _():
                remote(p_send.at[slot], p_recv.at[chip], PARTIAL, to).start()

            @pl.when(to == me)
            def _():
                local(p_send.at[slot], p_recv.at[chip], recv_sems.at[PARTIAL]).start()

    u_first = user_at(0)
    local(keys_hbm.at[u_first], k_buf.at[u_first], kv_sems.at[0, 0]).wait()
    set_queries(u_first)
    highest = lowest
    for j in range(length // CHUNK):
        highest = scores(u_first, j, s_even, highest)

    def two_users(i, highest):
        t = 2 * i

        @pl.when(i == half_users // 2 - 1)
        def _():
            pass_on(second_half)

        highest = attend(t, s_even, s_odd, highest)

        @pl.when(i > 0)
        def _():
            merge(t - 1)

        @pl.when(i == half_users // 2 - 1)
        def _():
            make_queries(second_half)
            xf[...] = x_buf[second_half].reshape(2 * nc * 16, width).astype(F32)

        highest = attend(t + 1, s_odd, s_even, highest)
        merge(t)
        return highest

    highest = lax.fori_loop(0, users // 2 - 1, two_users, highest)
    highest = attend(users - 2, s_even, s_odd, highest)
    merge(users - 3)
    attend(users - 1, s_odd, None, highest, more=False)
    merge(users - 2)
    merge(users - 1)

    wait_recv(p_recv, PARTIAL)
    ej = lax.broadcasted_iota(jnp.int32, (width, 4 * width), 0)
    ef = lax.broadcasted_iota(jnp.int32, (width, 4 * width), 1)
    same = (ej // head_size == lax.rem(ef, width) // head_size) & (
        lax.rem(ej, head_size) // 8 == ef // width
    )
    spread = jnp.where(same & (lax.rem(ej, 8) == 0), 1.0, 0.0).astype(BF16)
    spread_click = jnp.where(same & (lax.rem(ej, 8) == 1), 1.0, 0.0).astype(BF16)
    tiles = p_recv[:, 32:40, :]
    rest = tiles.reshape(nc * 8, width)
    lse_all = jnp.zeros((nc * 8, 4 * width), F32)
    for _ in range(3):
        piece = rest.astype(BF16)
        rest = rest - piece.astype(F32)
        lse_all = lse_all + jnp.dot(piece, spread, preferred_element_type=F32)
    lse_all = lse_all.reshape(nc, 8, 4 * width)
    w = jnp.exp2(lse_all - jnp.max(lse_all, axis=0)[None])
    den = jnp.sum(w, axis=0)
    attended = []
    for g in range(4):
        cols = slice(g * width, g * width + width)
        num = jnp.sum(p_recv[:, 8 * g : 8 * g + 8, :] * w[:, :, cols], axis=0)
        attended.append(num / den[:, cols])
    attended = jnp.concatenate(attended, axis=0).astype(BF16).astype(F32)
    click_tile = jnp.where(is_click, jnp.sum(tiles, axis=0), 0.0)
    click = jnp.dot(click_tile.astype(BF16), spread_click, preferred_element_type=F32)
    click = jnp.concatenate([click[:, g * width : g * width + width] for g in range(4)], axis=0)
    click = click[:, 0:1]

    def candidates_of(which):
        first = which * nc * 16 + lax.rem(u_me, half_users) * 2 + c_me
        return xf[pl.ds(first, nc, stride=16), :]

    features = jnp.concatenate([candidates_of(core), attended], axis=1)
    wh_load.wait()
    wout_load.wait()
    pre = jnp.dot(features.astype(BF16), wh_buf[...], preferred_element_type=F32)
    hidden = jnp.maximum(pre, 0.0).astype(BF16).astype(F32)
    logits = jnp.sum(hidden * wout_ref[...], axis=-1, keepdims=True)
    dlogit = 1.0 / (1.0 + jnp.exp(-logits)) - click
    h_send[0:32] = attended
    h_send[32:64] = jnp.broadcast_to(dlogit, (nc, width))
    remote(h_send, h_recv, TWIN_HEAD, twin).start()

    half_hid = wh_buf.shape[1] // 2
    my_cols = pl.ds(pl.multiple_of(core * half_hid, half_hid), half_hid)
    wout = wout_ref[:, my_cols]

    def half_of(a):
        return jnp.where(core == 0, a[:, :half_hid], a[:, half_hid:])

    def dpre_of(pre, dlogit):
        return jnp.where(pre > 0.0, dlogit * wout, 0.0).astype(BF16)

    dpre = dpre_of(half_of(pre), dlogit)
    out_part = jnp.sum(half_of(hidden) * dlogit, axis=0, keepdims=True)
    wait_recv(h_recv, TWIN_HEAD)
    other = jnp.concatenate([candidates_of(1 - core), h_recv[0:32]], axis=1)
    dlogit = h_recv[32:64, 0:1]
    pre = jnp.dot(other.astype(BF16), wh_buf[:, my_cols], preferred_element_type=F32)
    hidden = jnp.maximum(pre, 0.0).astype(BF16).astype(F32)
    out_part = out_part + jnp.sum(hidden * dlogit, axis=0, keepdims=True)
    features = jnp.concatenate([features, other], axis=0)
    dpre = jnp.concatenate([dpre, dpre_of(pre, dlogit)], axis=0)
    grad = jnp.dot(jnp.transpose(features).astype(BF16), dpre, preferred_element_type=F32)
    bw = half_hid // 2
    for part in range(2):
        for b in range(nc):
            i, j = b // 2, b % 2
            first = bw * j + width * part
            g_send[part, b] = grad[16 * i : 16 * i + 16, first : first + width].astype(BF16)

        @pl.loop(1, nc)
        def _(k):
            to = on_chip(k)
            remote(
                g_send.at[part, to], g_recv.at[part, chip], REDUCE + part, same_core(to)
            ).start()

        g_recv[part, chip] = g_send[part, chip]

    at_x, at_zy = lax.rem(chip, 4), chip // 4
    pieces = [out_part[:, width * i : width * i + width] for i in range(4)]
    o1[at_x] = jnp.concatenate(pieces + [jnp.zeros((4, width), F32)], axis=0)
    for k in range(1, 4):
        to = at_zy * 4 + lax.rem(at_x + k, 4)
        remote(o1.at[at_x], o1.at[at_x], OUT_X, same_core(to)).start()

    wait_recv(o1.at[pl.ds(0, 3)], OUT_X)
    o2[grp] = o1[0] + o1[1] + o1[2] + o1[3]
    for k in range(1, ng):
        remote(o2.at[grp], o2.at[grp], OUT_GRP, me, lax.rem(grp + k, ng)).start()
    for part in range(2):
        wait_recv(g_recv.at[part, pl.ds(0, nc - 1)], REDUCE + part)
        z_buf[part, grp] = jnp.sum(g_recv[part].astype(F32), axis=0).astype(BF16)
        for k in range(1, ng):
            block = z_buf.at[part, grp]
            remote(block, block, GRP + part, me, lax.rem(grp + k, ng)).start()
    wait_recv(o2.at[pl.ds(0, ng - 1)], OUT_GRP)
    o3[at_zy] = jnp.sum(o2[...], axis=0)
    for k in range(1, 8):
        to = lax.rem(at_zy + k, 8) * 4 + at_x
        remote(o3.at[at_zy], o3.at[at_zy], OUT_ZY, same_core(to)).start()
    wide = jnp.broadcast_to(logits, (nc, width))
    for i in range(nc):
        l_send[i] = wide[i : i + 1, :]
    l_slot = c_me * users + u_me

    @pl.loop(1, nc)
    def _(k):
        to = on_chip(k)
        remote(l_send.at[to], l_recv.at[l_slot], LOGITS, same_core(to)).start()

    l_recv[l_slot] = l_send[chip]

    for part in range(2):
        wait_recv(z_buf.at[part, pl.ds(0, ng - 1)], GRP + part)
        ga_buf[part, core, chip] = jnp.sum(z_buf[part].astype(F32), axis=0).astype(BF16)

        @pl.loop(1, nc)
        def _(k):
            block = ga_buf.at[part, core, chip]
            remote(block, block, ALL + part, same_core(on_chip(k))).start()

    wait_recv(l_recv.at[pl.ds(0, nc - 1)], LOGITS)
    logit_rows = l_recv[...].reshape(2 * users, width)
    row_o = lax.broadcasted_iota(jnp.int32, (users, width), 0)
    col_o = lax.broadcasted_iota(jnp.int32, (users, width), 1)
    for c in range(2):
        rows = jnp.where(row_o == col_o, logit_rows[users * c : users * (c + 1)], 0.0)
        logits_ref[c : c + 1, :] = jnp.sum(rows, axis=0, keepdims=True)[:, :users]
    wait_recv(o3.at[pl.ds(0, 7)], OUT_ZY)
    o4[core] = jnp.sum(o3[...], axis=0)
    remote(o4.at[core], o4.at[core], OUT_TWIN, twin).start()

    for part in range(2):
        wait_send(x_buf.at[0, pl.ds(0, nc - 1)], GATHER + part)
        wait_send(x_buf.at[0, pl.ds(0, nc)], GATHER_TWIN + part)
    local(theirs, theirs, twin_send_sem).wait()
    wait_send(p_send.at[pl.ds(0, nc - 1)], PARTIAL)
    wait_send(h_send, TWIN_HEAD)
    wait_send(l_send.at[pl.ds(0, nc - 1)], LOGITS)
    for part in range(2):
        wait_send(g_send.at[part, pl.ds(0, nc - 1)], REDUCE + part)
        wait_send(z_buf.at[part, pl.ds(0, ng - 1)], GRP + part)
    wait_send(o1.at[pl.ds(0, 3)], OUT_X)
    wait_send(o2.at[pl.ds(0, ng - 1)], OUT_GRP)
    wait_send(o3.at[pl.ds(0, 7)], OUT_ZY)

    def write(part, side):
        for j in range(2):
            first = side * half_hid + j * bw + part * width
            cols = pl.ds(pl.multiple_of(first, width), width)
            for i in range(nc // 2):
                gh_ref[16 * i : 16 * i + 16, cols] = ga_buf[part, side, 2 * i + j].astype(F32)

    for part in range(2):
        wait_recv(ga_buf.at[part, 0, pl.ds(0, nc - 1)], ALL + part)
        block = ga_buf.at[part, core]
        remote(block, block, ALL_TWIN + part, twin).start()
        write(part, core)
    wait_recv(o4.at[0], OUT_TWIN)
    go_ref[...] = jnp.concatenate([o4[0, 0:4], o4[1, 0:4]], axis=0)
    for part in range(2):
        wait_recv(ga_buf.at[part, 0], ALL_TWIN + part)
        write(part, 1 - core)
    for part in range(2):
        wait_send(ga_buf.at[part, 0, pl.ds(0, nc - 1)], ALL + part)
        wait_send(ga_buf.at[part, 0], ALL_TWIN + part)
    wait_send(o4.at[0], OUT_TWIN)


def on_device(ns, ng, candidates, behav_keys, behav_values, w_query, w_hidden, w_out, clicks):
    users, per_dev, width = candidates.shape
    length = behav_keys.shape[1]
    feats, hid = w_hidden.shape
    nc = ns // 2
    hbm_spec = pl.BlockSpec(memory_space=pltpu.HBM)
    vmem_spec = pl.BlockSpec(memory_space=pltpu.VMEM)
    logits, grad_hidden, grad_out = pl.pallas_call(
        functools.partial(kernel, nc, ng),
        out_shape=(
            jax.ShapeDtypeStruct((per_dev, users), F32),
            jax.ShapeDtypeStruct((feats, hid), F32),
            jax.ShapeDtypeStruct((8, width), F32),
        ),
        in_specs=[hbm_spec] * 7,
        out_specs=(vmem_spec, vmem_spec, vmem_spec),
        scratch_shapes=[
            pltpu.VMEM((2, ns, 16, width), BF16),
            pltpu.VMEM((ns * 16, width), F32),
            pltpu.VMEM((2, ns * 16, width), F32),
            pltpu.VMEM((users, length, width), BF16),
            pltpu.VMEM((users, length, width), BF16),
            pltpu.VMEM((length, HEADS * width), F32),
            pltpu.VMEM((length, HEADS * width), F32),
            pltpu.VMEM((HEADS * width, width), BF16),
            pltpu.VMEM((width, width), BF16),
            pltpu.VMEM((feats, hid), BF16),
            pltpu.VMEM((1, hid), F32),
            pltpu.VMEM((per_dev, users), jnp.int32),
            pltpu.VMEM((per_dev, users, width), F32),
            pltpu.VMEM((users, 2, 2, 64, width), F32),
            pltpu.VMEM((users, 2, 64, width), F32),
            pltpu.VMEM((nc, 40, width), F32),
            pltpu.VMEM((nc, 40, width), F32),
            pltpu.VMEM((64, width), F32),
            pltpu.VMEM((64, width), F32),
            pltpu.VMEM((2, nc, 16, width), BF16),
            pltpu.VMEM((2, nc, 16, width), BF16),
            pltpu.VMEM((2, ng, 16, width), BF16),
            pltpu.VMEM((2, 2, nc, 16, width), BF16),
            pltpu.VMEM((nc, 1, width), F32),
            pltpu.VMEM((nc, 1, width), F32),
            pltpu.VMEM((4, 8, width), F32),
            pltpu.VMEM((ng, 8, width), F32),
            pltpu.VMEM((8, 8, width), F32),
            pltpu.VMEM((2, 8, width), F32),
            pltpu.SemaphoreType.DMA((2, users)),
            pltpu.SemaphoreType.DMA((6,)),
            pltpu.SemaphoreType.DMA((users,)),
            pltpu.SemaphoreType.DMA,
            pltpu.SemaphoreType.DMA((PHASES,)),
            pltpu.SemaphoreType.DMA((PHASES,)),
        ],
        compiler_params=pltpu.CompilerParams(
            collective_id=0, has_side_effects=True, vmem_limit_bytes=40 * 2**20
        ),
        name="ranker",
    )(
        *(
            pltpu.with_memory_space_constraint(operand, pltpu.HBM)
            for operand in (
                candidates.reshape(users * per_dev, width),
                behav_keys,
                behav_values,
                w_query,
                w_hidden,
                w_out.reshape(1, hid),
                jnp.transpose(clicks),
            )
        )
    )
    return jnp.transpose(logits), grad_hidden, grad_out.reshape(hid)


def solution(mesh):
    return jax.shard_map(
        functools.partial(on_device, mesh.shape["seq"], mesh.shape["grp"]),
        mesh=mesh,
        in_specs=(
            P("grp", "seq", None),
            P("grp", "seq", None),
            P("grp", "seq", None),
            P(),
            P(),
            P(),
            P("grp", "seq"),
        ),
        out_specs=(P("grp", "seq"), P(), P()),
        check_vma=False,
    )
```
